32 devices in a mesh: ctx: 8 (over z, x), ch: 4 (over y, core).
Axes of the slice: x: 2, y: 2, z: 4, core: 2. Of those that a mesh axis runs over, the one named last changes fastest.
Arguments:
- tokens: bfloat16 [1024, 4096], P('ctx'), may hold values from -6 to 6
- value_weight: bfloat16 [4096, 2048], P(None, 'ch'), may hold values from -0.09375 to 0.09375
- gate_rows: bfloat16 [1024, 2048], P('ctx', 'ch'), may hold values from -6 to 6
- filter_taps: bfloat16 [1024, 2048], P('ctx', 'ch'), may hold values from -0.1875 to 0.1875
- out_weight: bfloat16 [2048, 4096], P('ch'), may hold values from -0.1875 to 0.1875
Outputs:
- mixed_out: bfloat16 [1024, 4096], P('ctx', 'ch')
The draws below stay inside these ranges and needn't reach their ends.
All inputs are finite; a program needn't handle non-finite values.
Results may differ from the reference program's by a relative error of at most 0.0095.
Values may be sent and summed in bfloat16 or wider, within the bound.
No kernel may reach another device: no remote copies, remote signals or barrier semaphores. Data moves between devices by JAX's collectives and lax.ppermute only.
A program may use at most 64 MiB of HBM per device.

```python
import jax
import jax.numpy as jnp
from jax import lax

D = 4096
C_DEV = 512
TOKENS = 1024
CHANNELS = 2048


def strengthened(array, key, source, target, shards_of, factor):
    def block_of(position):
        return (jnp.arange(array.shape[position]) // (array.shape[position] // shards_of)).reshape((-1,) + (1,) * (array.ndim - 1 - position))

    one_side = jax.random.permutation(key, shards_of)[block_of(target)]
    other_side = (block_of(target) + shards_of // 2) % shards_of
    return jnp.where((block_of(source) == one_side) | (block_of(source) == other_side), factor * array, array)


def block_scale(key, dims, shards, low, high):
    gain, own = 1.0, jax.random.fold_in(key, 6)
    for axis_at, shards_of in shards:
        steps = jnp.exp(jax.random.uniform(jax.random.fold_in(own, axis_at), (shards_of,), jnp.float32, low / len(shards), high / len(shards)))
        gain = gain * jnp.repeat(steps, dims[axis_at] // shards_of).reshape([-1 if axis == axis_at else 1 for axis in range(len(dims))])
    return gain


def normal_values(rng, shape, spread, most, shards=(), kind=jnp.bfloat16):
    factor_of = block_scale(rng, shape, shards, -0.22, 0.18) if shards else 1.0
    result = jax.random.normal(rng, shape, jnp.float32) * spread * factor_of
    return jnp.minimum(jnp.maximum(result, -most), most).astype(kind)


def gaussian_with(own_key, extent, scale, bound, shards, heavy, dtype=jnp.bfloat16):
    entries = scale * jax.random.normal(own_key, extent, jnp.float32)
    if shards:
        entries = entries * block_scale(own_key, extent, shards, -0.22, 0.18)
    return jnp.clip(strengthened(entries, jax.random.fold_in(own_key, 3), *heavy), -bound, bound).astype(dtype)


def setup_inputs(seed: int = 0) -> dict:
    streams_of = jax.random.split(jax.random.key(seed), 6)
    tokens = normal_values(streams_of[0], (TOKENS, D), 1.0, 6.0, ((0, 8),))
    value_weight = normal_values(streams_of[1], (D, CHANNELS), D ** -0.5, 0.09375, ((1, 4),))
    gate_rows = normal_values(streams_of[2], (TOKENS, CHANNELS), 1.0, 6.0, ((0, 8), (1, 4)))
    filter_taps = normal_values(streams_of[3], (TOKENS, CHANNELS), TOKENS ** -0.5, 0.1875, ((0, 8), (1, 4)))
    out_weight = gaussian_with(streams_of[4], (CHANNELS, D), CHANNELS ** -0.5, 0.1875, ((0, 4),), (0, 1, 4, 2.0))
    return {"tokens": tokens, "value_weight": value_weight, "gate_rows": gate_rows, "filter_taps": filter_taps, "out_weight": out_weight}


def causal_block(pair):
    value_block, taps_block = pair
    length = value_block.shape[0]
    spectrum_value = jnp.fft.rfft(value_block.astype(jnp.float32), n=2 * length, axis=0)
    spectrum_taps = jnp.fft.rfft(taps_block.astype(jnp.float32), n=2 * length, axis=0)
    return jnp.fft.irfft(spectrum_value * spectrum_taps, n=2 * length, axis=0)[:length]


def reference(tokens, value_weight, gate_rows, filter_taps, out_weight):
    value_rows = jnp.dot(tokens, value_weight, preferred_element_type=jnp.float32).astype(jnp.bfloat16)
    groups = CHANNELS // C_DEV
    value_groups = value_rows.reshape(TOKENS, groups, C_DEV).transpose(1, 0, 2)
    taps_groups = filter_taps.reshape(TOKENS, groups, C_DEV).transpose(1, 0, 2)
    convolved = lax.map(causal_block, (value_groups, taps_groups))
    convolved = convolved.transpose(1, 0, 2).reshape(TOKENS, CHANNELS).astype(jnp.bfloat16)
    convolved = lax.optimization_barrier(convolved)
    gated_rows = (convolved.astype(jnp.float32) * gate_rows.astype(jnp.float32)).astype(jnp.bfloat16)
    summed = jnp.zeros((TOKENS, D), jnp.float32)
    for group_index in range(groups):
        lower = group_index * C_DEV
        partial_sum = jnp.dot(gated_rows[:, lower:lower + C_DEV], out_weight[lower:lower + C_DEV], preferred_element_type=jnp.float32).astype(jnp.bfloat16)
        partial_sum = lax.optimization_barrier(partial_sum)
        summed = summed + partial_sum.astype(jnp.float32)
    return summed.astype(jnp.bfloat16)
```

```python
import math

import jax
import jax.numpy as jnp
import numpy as np
from jax import lax
from jax.experimental import pallas as pl
from jax.experimental.pallas import tpu as pltpu
from jax.sharding import PartitionSpec as P

HIGHEST = lax.Precision.HIGHEST


def column_tables(half_rows, peer_count):
    rows_full = 2 * half_rows
    length = rows_full * peer_count
    outer_freq = jnp.arange(rows_full, dtype=jnp.int32)[:, None]
    outer_pos = jnp.arange(half_rows, dtype=jnp.int32)[None, :]
    first_angle = (
        -2.0 * math.pi / rows_full * (outer_freq * outer_pos % rows_full).astype(jnp.float32)
    )
    inner_pos = jnp.arange(peer_count, dtype=jnp.int32)[None, :]
    twist_angle = -2.0 * math.pi / length * (outer_freq * inner_pos % length).astype(jnp.float32)
    inner_index = jnp.arange(peer_count, dtype=jnp.int32)
    second_angle = (
        -2.0
        * math.pi
        / peer_count
        * (inner_index[:, None] * inner_index[None, :] % peer_count).astype(jnp.float32)
    )
    return (
        jnp.cos(first_angle),
        jnp.sin(first_angle),
        jnp.cos(twist_angle),
        jnp.sin(twist_angle),
        jnp.cos(second_angle),
        jnp.sin(second_angle),
    )


def column_spectrum(signal, tables):
    first_cos, first_sin, twist_cos, twist_sin, second_cos, second_sin = tables
    section_real = jnp.einsum("kn,nbc->ckb", first_cos, signal, precision=HIGHEST)
    section_imag = jnp.einsum("kn,nbc->ckb", first_sin, signal, precision=HIGHEST)
    turned_real = section_real * twist_cos - section_imag * twist_sin
    turned_imag = section_real * twist_sin + section_imag * twist_cos

    def apply_second(table_part, operand):
        return jnp.einsum("ckb,bj->ckj", operand, table_part, precision=HIGHEST)

    spec_real = apply_second(second_cos, turned_real) - apply_second(second_sin, turned_imag)
    spec_imag = apply_second(second_sin, turned_real) + apply_second(second_cos, turned_imag)
    return (spec_real, spec_imag)


def column_inverse(spec_real, spec_imag, tables):
    first_cos, first_sin, twist_cos, twist_sin, second_cos, second_sin = tables

    def apply_second(table_part, operand):
        return jnp.einsum("ckj,bj->ckb", operand, table_part, precision=HIGHEST)

    back_real = apply_second(second_cos, spec_real) + apply_second(second_sin, spec_imag)
    back_imag = apply_second(second_cos, spec_imag) - apply_second(second_sin, spec_real)
    turned_real = back_real * twist_cos + back_imag * twist_sin
    turned_imag = back_imag * twist_cos - back_real * twist_sin
    return jnp.einsum("kn,ckb->nbc", first_cos, turned_real, precision=HIGHEST) + jnp.einsum(
        "kn,ckb->nbc", first_sin, turned_imag, precision=HIGHEST
    )


def by_transform(tokens, value_weight, gate_rows, filter_taps, out_weight):
    local_rows = tokens.shape[0]
    peer_count = lax.axis_size("ctx")
    length = peer_count * local_rows
    value_rows = jnp.dot(tokens, value_weight, preferred_element_type=jnp.float32).astype(
        jnp.bfloat16
    )
    value_columns = lax.all_to_all(value_rows, "ctx", split_axis=1, concat_axis=0, tiled=True)
    tap_columns = lax.all_to_all(filter_taps, "ctx", split_axis=1, concat_axis=0, tiled=True)
    channels_here = value_columns.shape[1]
    tables = column_tables(local_rows, peer_count)
    value_signal = value_columns.astype(jnp.float32).reshape(local_rows, peer_count, channels_here)
    tap_signal = tap_columns.astype(jnp.float32).reshape(local_rows, peer_count, channels_here)
    value_real, value_imag = column_spectrum(value_signal, tables)
    tap_real, tap_imag = column_spectrum(tap_signal, tables)
    product_real = value_real * tap_real - value_imag * tap_imag
    product_imag = value_real * tap_imag + value_imag * tap_real
    restored = column_inverse(product_real, product_imag, tables) / (2.0 * length)
    restored = restored.reshape(length, channels_here).astype(jnp.bfloat16)
    convolved = lax.all_to_all(restored, "ctx", split_axis=0, concat_axis=1, tiled=True)
    gated_rows = (convolved.astype(jnp.float32) * gate_rows.astype(jnp.float32)).astype(
        jnp.bfloat16
    )
    partial_sum = jnp.dot(gated_rows, out_weight, preferred_element_type=jnp.float32)
    own_sum = lax.psum_scatter(
        partial_sum.astype(jnp.bfloat16), "ch", scatter_dimension=1, tiled=True
    )
    return own_sum


LANES = 128
SHIFTS = 16
GROUP = 16
NT = (((1,), (1,)), ((), ()))
TN = (((0,), (0,)), ((), ()))


def value_kernel(tokens_ref, weight_ref, taps_ref, gate_ref, payload_ref, gate_t_ref, total_ref):
    step = pl.program_id(0)
    peers, both, rows = payload_ref.shape
    part = both // 2

    @pl.when(step == 0)
    def _():
        total_ref[...] = jnp.zeros_like(total_ref)
        row = lax.broadcasted_iota(jnp.int32, (rows, rows), 0)
        column = lax.broadcasted_iota(jnp.int32, (rows, rows), 1)
        flip = jnp.where(row + column == rows - 1, 1.0, 0.0).astype(jnp.bfloat16)
        flipped = jnp.dot(flip, taps_ref[...], preferred_element_type=jnp.float32)
        flipped_t = flipped.T.astype(jnp.bfloat16)
        for peer in range(peers):
            payload_ref[peer, part:, :] = flipped_t[peer * part : (peer + 1) * part]
        gate_t_ref[...] = gate_ref[...].astype(jnp.float32).T.astype(jnp.bfloat16)

    total_ref[...] += jnp.dot(
        tokens_ref[...], weight_ref[...], preferred_element_type=jnp.float32
    )

    @pl.when(step == pl.num_programs(0) - 1)
    def _():
        value_t = total_ref[...].T.astype(jnp.bfloat16)
        for peer in range(peers):
            payload_ref[peer, :part, :] = value_t[peer * part : (peer + 1) * part]


def value_payload(tokens, value_weight, filter_taps, gate_rows, peers):
    rows, depth = tokens.shape
    channels = value_weight.shape[1]
    steps = 4
    block = depth // steps
    return pl.pallas_call(
        value_kernel,
        grid=(steps,),
        in_specs=[
            pl.BlockSpec((rows, block), lambda k: (0, k)),
            pl.BlockSpec((block, channels), lambda k: (k, 0)),
            pl.BlockSpec((rows, channels), lambda k: (0, 0)),
            pl.BlockSpec((rows, channels), lambda k: (0, 0)),
        ],
        out_specs=[
            pl.BlockSpec((peers, 2 * channels // peers, rows), lambda k: (0, 0, 0)),
            pl.BlockSpec((channels, rows), lambda k: (0, 0)),
        ],
        out_shape=[
            jax.ShapeDtypeStruct((peers, 2 * channels // peers, rows), jnp.bfloat16),
            jax.ShapeDtypeStruct((channels, rows), jnp.bfloat16),
        ],
        scratch_shapes=[pltpu.VMEM((rows, channels), jnp.float32)],
        compiler_params=pltpu.CompilerParams(vmem_limit_bytes=16 * 2**20),
    )(tokens, value_weight, filter_taps, gate_rows)


def conv_kernel(payload_ref, place_ref, out_ref, value_ref, taps_ref, picked_ref):
    blocks, both, lanes = payload_ref.shape
    channels = both // 2
    length = blocks * lanes
    outer = lanes // SHIFTS
    tail = jnp.zeros((GROUP, lanes), jnp.float32)
    rows = 2 * outer * GROUP
    row = lax.broadcasted_iota(jnp.int32, (rows, SHIFTS * GROUP), 0)
    column = lax.broadcasted_iota(jnp.int32, (rows, SHIFTS * GROUP), 1)
    same = row % GROUP == column % GROUP
    for group in range(channels // GROUP):
        first = group * GROUP
        padded = jnp.concatenate(
            [
                payload_ref[q, first : first + GROUP, :].astype(jnp.float32)
                for q in range(blocks)
            ]
            + [tail],
            axis=1,
        )
        for shift in range(SHIFTS):
            moved = pltpu.roll(padded, shift, 1) if shift else padded
            value_ref[group, shift * GROUP : (shift + 1) * GROUP, :] = moved[:, :length].astype(
                jnp.bfloat16
            )
        padded = jnp.concatenate(
            [
                payload_ref[blocks - 1 - q, channels + first : channels + first + GROUP, :].astype(
                    jnp.float32
                )
                for q in range(blocks)
            ]
            + [tail],
            axis=1,
        )
        for k in range(outer):
            left = SHIFTS * (outer - 1 - k)
            moved = pltpu.roll(padded, length + lanes - left, 1) if left else padded
            taps_ref[group, k * GROUP : (k + 1) * GROUP, :length] = moved[:, :length].astype(
                jnp.bfloat16
            )
        taps_ref[group, :, length:] = jnp.zeros((outer * GROUP, lanes), jnp.bfloat16)
        for pair in range(blocks // 2):
            depth = 2 * lanes * (pair + 1)
            even = (blocks - 1 - 2 * pair) * lanes
            odd = even - lanes
            left_side = jnp.concatenate(
                [
                    taps_ref[group, :, even : even + depth],
                    taps_ref[group, :, odd : odd + depth],
                ],
                axis=0,
            )
            mixed = lax.dot_general(
                left_side, value_ref[group, :, :depth], NT, preferred_element_type=jnp.float32
            )
            picked = jnp.where(same, mixed, 0.0).astype(jnp.bfloat16)
            for half in range(2):
                block = 2 * pair + half
                for k in range(outer):
                    at = (half * outer + k) * GROUP
                    picked_ref[
                        group,
                        block * GROUP : (block + 1) * GROUP,
                        k * SHIFTS * GROUP : (k + 1) * SHIFTS * GROUP,
                    ] = picked[at : at + GROUP]
        result = jnp.dot(picked_ref[group], place_ref[...], preferred_element_type=jnp.float32)
        result = result.astype(jnp.bfloat16)
        for block in range(blocks):
            out_ref[block, first : first + GROUP, :] = result[block * GROUP : (block + 1) * GROUP]


def placement(lanes):
    outer = lanes // SHIFTS
    k, r, _, t = np.ix_(range(outer), range(SHIFTS), range(GROUP), range(lanes))
    hit = np.broadcast_to(t == SHIFTS * k + SHIFTS - 1 - r, (outer, SHIFTS, GROUP, lanes))
    return jnp.asarray(hit.reshape(outer * SHIFTS * GROUP, lanes), jnp.bfloat16)


def convolve(payload):
    blocks, both, lanes = payload.shape
    channels = both // 2
    groups = channels // GROUP
    outer = lanes // SHIFTS
    return pl.pallas_call(
        conv_kernel,
        out_shape=jax.ShapeDtypeStruct((blocks, channels, lanes), jnp.bfloat16),
        scratch_shapes=[
            pltpu.VMEM((groups, SHIFTS * GROUP, blocks * lanes), jnp.bfloat16),
            pltpu.VMEM((groups, outer * GROUP, (blocks + 1) * lanes), jnp.bfloat16),
            pltpu.VMEM((groups, blocks * GROUP, outer * SHIFTS * GROUP), jnp.bfloat16),
        ],
        compiler_params=pltpu.CompilerParams(vmem_limit_bytes=24 * 2**20),
    )(payload, placement(lanes))


def gate_kernel(conv_ref, gate_ref, out_ref):
    out_ref[...] = (
        conv_ref[...].astype(jnp.float32) * gate_ref[...].astype(jnp.float32)
    ).astype(out_ref.dtype)


def gated(conv_t, gate_t):
    return pl.pallas_call(
        gate_kernel,
        out_shape=jax.ShapeDtypeStruct(conv_t.shape, jnp.bfloat16),
        compiler_params=pltpu.CompilerParams(vmem_limit_bytes=4 * 2**20),
    )(conv_t, gate_t)


def project_kernel(at_ref, own_ref, other_ref, own_weight_ref, other_weight_ref, out_ref):
    total = lax.dot_general(
        own_ref[...], own_weight_ref[...], TN, preferred_element_type=jnp.float32
    )
    total += lax.dot_general(
        other_ref[...], other_weight_ref[...], TN, preferred_element_type=jnp.float32
    )
    out_ref[...] = total.astype(out_ref.dtype)


def project(at, own, other, own_weight, other_weight, features, dtype):
    depth, rows = own.shape
    steps = 4
    block = features // steps
    return pl.pallas_call(
        project_kernel,
        grid_spec=pltpu.PrefetchScalarGridSpec(
            num_scalar_prefetch=1,
            grid=(steps,),
            in_specs=[
                pl.BlockSpec((depth, rows), lambda n, at: (0, 0)),
                pl.BlockSpec((depth, rows), lambda n, at: (0, 0)),
                pl.BlockSpec((depth, block), lambda n, at: (0, at[0] * steps + n)),
                pl.BlockSpec((depth, block), lambda n, at: (0, at[0] * steps + n)),
            ],
            out_specs=pl.BlockSpec((rows, block), lambda n, at: (0, n)),
        ),
        out_shape=jax.ShapeDtypeStruct((rows, features), dtype),
        compiler_params=pltpu.CompilerParams(vmem_limit_bytes=16 * 2**20),
    )(at, own, other, own_weight, other_weight)


def by_blocks(tokens, value_weight, gate_rows, filter_taps, out_weight):
    peers = lax.axis_size("ctx")
    ranks = lax.axis_size("ch")
    rank = lax.axis_index("ch")
    features = out_weight.shape[1] // ranks
    near = [(i, i ^ 1) for i in range(ranks)]
    far = [(i, i ^ 2) for i in range(ranks)]
    other_weight = lax.ppermute(out_weight, "ch", near)
    payload, gate_t = value_payload(tokens, value_weight, filter_taps, gate_rows, peers)
    payload = lax.all_to_all(payload, "ctx", split_axis=0, concat_axis=0, tiled=True)
    conv = convolve(payload)
    conv = lax.all_to_all(conv, "ctx", split_axis=0, concat_axis=0, tiled=True)
    own = gated(conv.reshape(gate_t.shape), gate_t)
    other = lax.ppermute(own, "ch", near)
    far_at, own_at = (rank ^ 2)[None], rank[None]
    sent = project(far_at, own, other, out_weight, other_weight, features, jnp.bfloat16)
    arrived = lax.ppermute(sent, "ch", far)
    kept = project(own_at, own, other, out_weight, other_weight, features, jnp.float32)
    return (kept + arrived.astype(jnp.float32)).astype(jnp.bfloat16)


def fits_blocks(tokens, value_weight, peers, ranks):
    rows, channels = tokens.shape[0], value_weight.shape[1]
    return (
        rows == LANES
        and ranks == 4
        and peers % 2 == 0
        and peers <= 16
        and channels % (peers * GROUP) == 0
    )


def on_device(tokens, value_weight, gate_rows, filter_taps, out_weight):
    peers, ranks = lax.axis_size("ctx"), lax.axis_size("ch")
    if fits_blocks(tokens, value_weight, peers, ranks):
        return by_blocks(tokens, value_weight, gate_rows, filter_taps, out_weight)
    return by_transform(tokens, value_weight, gate_rows, filter_taps, out_weight)


def solution(mesh):
    placed = (P("ctx", None), P(None, "ch"), P("ctx", "ch"), P("ctx", "ch"), P("ch", None))
    return jax.shard_map(
        on_device, mesh=mesh, in_specs=placed, out_specs=P("ctx", "ch"), check_vma=False
    )
```

```python
import functools
import math

import jax
import jax.numpy as jnp
import numpy as np
from jax import lax
from jax.experimental import pallas as pl
from jax.experimental.pallas import tpu as pltpu
from jax.sharding import PartitionSpec as P

HIGHEST = lax.Precision.HIGHEST


def column_tables(half_rows, peer_count):
    rows_full = 2 * half_rows
    length = rows_full * peer_count
    outer_freq = jnp.arange(rows_full, dtype=jnp.int32)[:, None]
    outer_pos = jnp.arange(half_rows, dtype=jnp.int32)[None, :]
    first_angle = (
        -2.0 * math.pi / rows_full * (outer_freq * outer_pos % rows_full).astype(jnp.float32)
    )
    inner_pos = jnp.arange(peer_count, dtype=jnp.int32)[None, :]
    twist_angle = -2.0 * math.pi / length * (outer_freq * inner_pos % length).astype(jnp.float32)
    inner_index = jnp.arange(peer_count, dtype=jnp.int32)
    second_angle = (
        -2.0
        * math.pi
        / peer_count
        * (inner_index[:, None] * inner_index[None, :] % peer_count).astype(jnp.float32)
    )
    return (
        jnp.cos(first_angle),
        jnp.sin(first_angle),
        jnp.cos(twist_angle),
        jnp.sin(twist_angle),
        jnp.cos(second_angle),
        jnp.sin(second_angle),
    )


def column_spectrum(signal, tables):
    first_cos, first_sin, twist_cos, twist_sin, second_cos, second_sin = tables
    section_real = jnp.einsum("kn,nbc->ckb", first_cos, signal, precision=HIGHEST)
    section_imag = jnp.einsum("kn,nbc->ckb", first_sin, signal, precision=HIGHEST)
    turned_real = section_real * twist_cos - section_imag * twist_sin
    turned_imag = section_real * twist_sin + section_imag * twist_cos

    def apply_second(table_part, operand):
        return jnp.einsum("ckb,bj->ckj", operand, table_part, precision=HIGHEST)

    spec_real = apply_second(second_cos, turned_real) - apply_second(second_sin, turned_imag)
    spec_imag = apply_second(second_sin, turned_real) + apply_second(second_cos, turned_imag)
    return (spec_real, spec_imag)


def column_inverse(spec_real, spec_imag, tables):
    first_cos, first_sin, twist_cos, twist_sin, second_cos, second_sin = tables

    def apply_second(table_part, operand):
        return jnp.einsum("ckj,bj->ckb", operand, table_part, precision=HIGHEST)

    back_real = apply_second(second_cos, spec_real) + apply_second(second_sin, spec_imag)
    back_imag = apply_second(second_cos, spec_imag) - apply_second(second_sin, spec_real)
    turned_real = back_real * twist_cos + back_imag * twist_sin
    turned_imag = back_imag * twist_cos - back_real * twist_sin
    return jnp.einsum("kn,ckb->nbc", first_cos, turned_real, precision=HIGHEST) + jnp.einsum(
        "kn,ckb->nbc", first_sin, turned_imag, precision=HIGHEST
    )


def by_transform(tokens, value_weight, gate_rows, filter_taps, out_weight):
    local_rows = tokens.shape[0]
    peer_count = lax.axis_size("ctx")
    length = peer_count * local_rows
    value_rows = jnp.dot(tokens, value_weight, preferred_element_type=jnp.float32).astype(
        jnp.bfloat16
    )
    value_columns = lax.all_to_all(value_rows, "ctx", split_axis=1, concat_axis=0, tiled=True)
    tap_columns = lax.all_to_all(filter_taps, "ctx", split_axis=1, concat_axis=0, tiled=True)
    channels_here = value_columns.shape[1]
    tables = column_tables(local_rows, peer_count)
    value_signal = value_columns.astype(jnp.float32).reshape(local_rows, peer_count, channels_here)
    tap_signal = tap_columns.astype(jnp.float32).reshape(local_rows, peer_count, channels_here)
    value_real, value_imag = column_spectrum(value_signal, tables)
    tap_real, tap_imag = column_spectrum(tap_signal, tables)
    product_real = value_real * tap_real - value_imag * tap_imag
    product_imag = value_real * tap_imag + value_imag * tap_real
    restored = column_inverse(product_real, product_imag, tables) / (2.0 * length)
    restored = restored.reshape(length, channels_here).astype(jnp.bfloat16)
    convolved = lax.all_to_all(restored, "ctx", split_axis=0, concat_axis=1, tiled=True)
    gated_rows = (convolved.astype(jnp.float32) * gate_rows.astype(jnp.float32)).astype(
        jnp.bfloat16
    )
    partial_sum = jnp.dot(gated_rows, out_weight, preferred_element_type=jnp.float32)
    own_sum = lax.psum_scatter(
        partial_sum.astype(jnp.bfloat16), "ch", scatter_dimension=1, tiled=True
    )
    return own_sum


LANES = 128
SHIFTS = 16
GROUP = 16
NT = (((1,), (1,)), ((), ()))
TN = (((0,), (0,)), ((), ()))


def turn_kernel(value_ref, taps_ref, gate_ref, payload_ref, gate_t_ref):
    peers, both, rows = payload_ref.shape
    part = both // 2
    row = lax.broadcasted_iota(jnp.int32, (rows, rows), 0)
    column = lax.broadcasted_iota(jnp.int32, (rows, rows), 1)
    flip = jnp.where(row + column == rows - 1, 1.0, 0.0).astype(jnp.bfloat16)
    flipped = jnp.dot(flip, taps_ref[...], preferred_element_type=jnp.float32)
    flipped_t = flipped.T.astype(jnp.bfloat16)
    value_t = value_ref[...].astype(jnp.float32).T.astype(jnp.bfloat16)
    for peer in range(peers):
        payload_ref[peer, :part, :] = value_t[peer * part : (peer + 1) * part]
        payload_ref[peer, part:, :] = flipped_t[peer * part : (peer + 1) * part]
    gate_t_ref[...] = gate_ref[...].astype(jnp.float32).T.astype(jnp.bfloat16)


def turned(value, filter_taps, gate_rows, peers):
    rows, channels = value.shape
    return pl.pallas_call(
        turn_kernel,
        out_shape=[
            jax.ShapeDtypeStruct((peers, 2 * channels // peers, rows), jnp.bfloat16),
            jax.ShapeDtypeStruct((channels, rows), jnp.bfloat16),
        ],
        compiler_params=pltpu.CompilerParams(vmem_limit_bytes=8 * 2**20),
    )(value, filter_taps, gate_rows)


def conv_kernel(payload_ref, place_ref, out_ref, value_ref, taps_ref, picked_ref):
    blocks, both, lanes = payload_ref.shape
    channels = both // 2
    length = blocks * lanes
    outer = lanes // SHIFTS
    tail = jnp.zeros((GROUP, lanes), jnp.float32)
    rows = 2 * outer * GROUP
    row = lax.broadcasted_iota(jnp.int32, (rows, SHIFTS * GROUP), 0)
    column = lax.broadcasted_iota(jnp.int32, (rows, SHIFTS * GROUP), 1)
    same = row % GROUP == column % GROUP
    for group in range(channels // GROUP):
        first = group * GROUP
        padded = jnp.concatenate(
            [
                payload_ref[q, first : first + GROUP, :].astype(jnp.float32)
                for q in range(blocks)
            ]
            + [tail],
            axis=1,
        )
        for shift in range(SHIFTS):
            moved = pltpu.roll(padded, shift, 1) if shift else padded
            value_ref[group, shift * GROUP : (shift + 1) * GROUP, :] = moved[:, :length].astype(
                jnp.bfloat16
            )
        padded = jnp.concatenate(
            [
                payload_ref[blocks - 1 - q, channels + first : channels + first + GROUP, :].astype(
                    jnp.float32
                )
                for q in range(blocks)
            ]
            + [tail],
            axis=1,
        )
        for k in range(outer):
            left = SHIFTS * (outer - 1 - k)
            moved = pltpu.roll(padded, length + lanes - left, 1) if left else padded
            taps_ref[group, k * GROUP : (k + 1) * GROUP, :length] = moved[:, :length].astype(
                jnp.bfloat16
            )
        taps_ref[group, :, length:] = jnp.zeros((outer * GROUP, lanes), jnp.bfloat16)
        for pair in range(blocks // 2):
            span = 2 * lanes * (pair + 1)
            even = (blocks - 1 - 2 * pair) * lanes
            odd = even - lanes
            left_side = jnp.concatenate(
                [
                    taps_ref[group, :, even : even + span],
                    taps_ref[group, :, odd : odd + span],
                ],
                axis=0,
            )
            mixed = lax.dot_general(
                left_side, value_ref[group, :, :span], NT, preferred_element_type=jnp.float32
            )
            picked = jnp.where(same, mixed, 0.0).astype(jnp.bfloat16)
            for half in range(2):
                block = 2 * pair + half
                for k in range(outer):
                    at = (half * outer + k) * GROUP
                    picked_ref[
                        group,
                        block * GROUP : (block + 1) * GROUP,
                        k * SHIFTS * GROUP : (k + 1) * SHIFTS * GROUP,
                    ] = picked[at : at + GROUP]
        result = jnp.dot(picked_ref[group], place_ref[...], preferred_element_type=jnp.float32)
        result = result.astype(jnp.bfloat16)
        for block in range(blocks):
            out_ref[block, first : first + GROUP, :] = result[block * GROUP : (block + 1) * GROUP]


def placement(lanes):
    outer = lanes // SHIFTS
    k, r, _, t = np.ix_(range(outer), range(SHIFTS), range(GROUP), range(lanes))
    hit = np.broadcast_to(t == SHIFTS * k + SHIFTS - 1 - r, (outer, SHIFTS, GROUP, lanes))
    return jnp.asarray(hit.reshape(outer * SHIFTS * GROUP, lanes), jnp.bfloat16)


def convolve(payload):
    blocks, both, lanes = payload.shape
    channels = both // 2
    groups = channels // GROUP
    outer = lanes // SHIFTS
    return pl.pallas_call(
        conv_kernel,
        out_shape=jax.ShapeDtypeStruct((blocks, channels, lanes), jnp.bfloat16),
        scratch_shapes=[
            pltpu.VMEM((groups, SHIFTS * GROUP, blocks * lanes), jnp.bfloat16),
            pltpu.VMEM((groups, outer * GROUP, (blocks + 1) * lanes), jnp.bfloat16),
            pltpu.VMEM((groups, blocks * GROUP, outer * SHIFTS * GROUP), jnp.bfloat16),
        ],
        cost_estimate=pl.CostEstimate(
            flops=2 * channels * GROUP * (blocks * lanes) ** 2,
            bytes_accessed=6 * channels * blocks * lanes,
            transcendentals=0,
        ),
        compiler_params=pltpu.CompilerParams(vmem_limit_bytes=24 * 2**20),
    )(payload, placement(lanes))


def gate_kernel(conv_ref, gate_ref, out_ref):
    out_ref[...] = (
        conv_ref[...].astype(jnp.float32) * gate_ref[...].astype(jnp.float32)
    ).astype(out_ref.dtype)


def gated(conv_t, gate_t):
    return pl.pallas_call(
        gate_kernel,
        out_shape=jax.ShapeDtypeStruct(conv_t.shape, jnp.bfloat16),
        compiler_params=pltpu.CompilerParams(vmem_limit_bytes=4 * 2**20),
    )(conv_t, gate_t)


def project_kernel(far, own_ref, other_ref, own_weight_ref, other_weight_ref, out_ref):
    features = out_ref.shape[1]
    rank = lax.axis_index("ch") ^ (2 if far else 0)
    span = pl.ds(pl.multiple_of(rank * features, features), features)
    total = lax.dot_general(
        own_ref[...], own_weight_ref[:, span], TN, preferred_element_type=jnp.float32
    )
    total += lax.dot_general(
        other_ref[...], other_weight_ref[:, span], TN, preferred_element_type=jnp.float32
    )
    out_ref[...] = total.astype(out_ref.dtype)


def project(own, other, own_weight, other_weight, features, far, dtype):
    return pl.pallas_call(
        functools.partial(project_kernel, far),
        out_shape=jax.ShapeDtypeStruct((own.shape[1], features), dtype),
        compiler_params=pltpu.CompilerParams(vmem_limit_bytes=24 * 2**20),
    )(own, other, own_weight, other_weight)


def by_blocks(tokens, value_weight, gate_rows, filter_taps, out_weight):
    peers = lax.axis_size("ctx")
    ranks = lax.axis_size("ch")
    features = out_weight.shape[1] // ranks
    near = [(i, i ^ 1) for i in range(ranks)]
    far = [(i, i ^ 2) for i in range(ranks)]
    value = jnp.dot(tokens, value_weight, preferred_element_type=jnp.float32).astype(
        jnp.bfloat16
    )
    payload, gate_t = turned(value, filter_taps, gate_rows, peers)
    other_weight = lax.ppermute(out_weight, "ch", near)
    payload = lax.all_to_all(payload, "ctx", split_axis=0, concat_axis=0, tiled=True)
    conv = convolve(payload)
    conv = lax.all_to_all(conv, "ctx", split_axis=0, concat_axis=0, tiled=True)
    own = gated(conv.reshape(gate_t.shape), gate_t)
    other = lax.ppermute(own, "ch", near)
    sent = project(own, other, out_weight, other_weight, features, True, jnp.bfloat16)
    arrived = lax.ppermute(sent, "ch", far)
    kept = project(own, other, out_weight, other_weight, features, False, jnp.float32)
    return (kept + arrived.astype(jnp.float32)).astype(jnp.bfloat16)


def fits_blocks(tokens, value_weight, peers, ranks):
    rows, channels = tokens.shape[0], value_weight.shape[1]
    return (
        rows == LANES
        and ranks == 4
        and peers % 2 == 0
        and peers <= 16
        and channels % (peers * GROUP) == 0
    )


def on_device(tokens, value_weight, gate_rows, filter_taps, out_weight):
    peers, ranks = lax.axis_size("ctx"), lax.axis_size("ch")
    if fits_blocks(tokens, value_weight, peers, ranks):
        return by_blocks(tokens, value_weight, gate_rows, filter_taps, out_weight)
    return by_transform(tokens, value_weight, gate_rows, filter_taps, out_weight)


def solution(mesh):
    placed = (P("ctx", None), P(None, "ch"), P("ctx", "ch"), P("ctx", "ch"), P("ch", None))
    return jax.shard_map(
        on_device, mesh=mesh, in_specs=placed, out_specs=P("ctx", "ch"), check_vma=False
    )
```

```python
import functools
import math

import jax
import jax.numpy as jnp
import numpy as np
from jax import lax
from jax.experimental import pallas as pl
from jax.experimental.pallas import tpu as pltpu
from jax.sharding import PartitionSpec as P

HIGHEST = lax.Precision.HIGHEST


def column_tables(half_rows, peer_count):
    rows_full = 2 * half_rows
    length = rows_full * peer_count
    outer_freq = jnp.arange(rows_full, dtype=jnp.int32)[:, None]
    outer_pos = jnp.arange(half_rows, dtype=jnp.int32)[None, :]
    first_angle = (
        -2.0 * math.pi / rows_full * (outer_freq * outer_pos % rows_full).astype(jnp.float32)
    )
    inner_pos = jnp.arange(peer_count, dtype=jnp.int32)[None, :]
    twist_angle = -2.0 * math.pi / length * (outer_freq * inner_pos % length).astype(jnp.float32)
    inner_index = jnp.arange(peer_count, dtype=jnp.int32)
    second_angle = (
        -2.0
        * math.pi
        / peer_count
        * (inner_index[:, None] * inner_index[None, :] % peer_count).astype(jnp.float32)
    )
    return (
        jnp.cos(first_angle),
        jnp.sin(first_angle),
        jnp.cos(twist_angle),
        jnp.sin(twist_angle),
        jnp.cos(second_angle),
        jnp.sin(second_angle),
    )


def column_spectrum(signal, tables):
    first_cos, first_sin, twist_cos, twist_sin, second_cos, second_sin = tables
    section_real = jnp.einsum("kn,nbc->ckb", first_cos, signal, precision=HIGHEST)
    section_imag = jnp.einsum("kn,nbc->ckb", first_sin, signal, precision=HIGHEST)
    turned_real = section_real * twist_cos - section_imag * twist_sin
    turned_imag = section_real * twist_sin + section_imag * twist_cos

    def apply_second(table_part, operand):
        return jnp.einsum("ckb,bj->ckj", operand, table_part, precision=HIGHEST)

    spec_real = apply_second(second_cos, turned_real) - apply_second(second_sin, turned_imag)
    spec_imag = apply_second(second_sin, turned_real) + apply_second(second_cos, turned_imag)
    return (spec_real, spec_imag)


def column_inverse(spec_real, spec_imag, tables):
    first_cos, first_sin, twist_cos, twist_sin, second_cos, second_sin = tables

    def apply_second(table_part, operand):
        return jnp.einsum("ckj,bj->ckb", operand, table_part, precision=HIGHEST)

    back_real = apply_second(second_cos, spec_real) + apply_second(second_sin, spec_imag)
    back_imag = apply_second(second_cos, spec_imag) - apply_second(second_sin, spec_real)
    turned_real = back_real * twist_cos + back_imag * twist_sin
    turned_imag = back_imag * twist_cos - back_real * twist_sin
    return jnp.einsum("kn,ckb->nbc", first_cos, turned_real, precision=HIGHEST) + jnp.einsum(
        "kn,ckb->nbc", first_sin, turned_imag, precision=HIGHEST
    )


def by_transform(tokens, value_weight, gate_rows, filter_taps, out_weight):
    local_rows = tokens.shape[0]
    peer_count = lax.axis_size("ctx")
    length = peer_count * local_rows
    value_rows = jnp.dot(tokens, value_weight, preferred_element_type=jnp.float32).astype(
        jnp.bfloat16
    )
    value_columns = lax.all_to_all(value_rows, "ctx", split_axis=1, concat_axis=0, tiled=True)
    tap_columns = lax.all_to_all(filter_taps, "ctx", split_axis=1, concat_axis=0, tiled=True)
    channels_here = value_columns.shape[1]
    tables = column_tables(local_rows, peer_count)
    value_signal = value_columns.astype(jnp.float32).reshape(local_rows, peer_count, channels_here)
    tap_signal = tap_columns.astype(jnp.float32).reshape(local_rows, peer_count, channels_here)
    value_real, value_imag = column_spectrum(value_signal, tables)
    tap_real, tap_imag = column_spectrum(tap_signal, tables)
    product_real = value_real * tap_real - value_imag * tap_imag
    product_imag = value_real * tap_imag + value_imag * tap_real
    restored = column_inverse(product_real, product_imag, tables) / (2.0 * length)
    restored = restored.reshape(length, channels_here).astype(jnp.bfloat16)
    convolved = lax.all_to_all(restored, "ctx", split_axis=0, concat_axis=1, tiled=True)
    gated_rows = (convolved.astype(jnp.float32) * gate_rows.astype(jnp.float32)).astype(
        jnp.bfloat16
    )
    partial_sum = jnp.dot(gated_rows, out_weight, preferred_element_type=jnp.float32)
    own_sum = lax.psum_scatter(
        partial_sum.astype(jnp.bfloat16), "ch", scatter_dimension=1, tiled=True
    )
    return own_sum


LANES = 128
SHIFTS = 16
GROUP = 16
NT = (((1,), (1,)), ((), ()))
TN = (((0,), (0,)), ((), ()))


def turn_kernel(value_ref, taps_ref, gate_ref, payload_ref, gate_t_ref):
    peers, both, rows = payload_ref.shape
    part = both // 2
    row = lax.broadcasted_iota(jnp.int32, (rows, rows), 0)
    column = lax.broadcasted_iota(jnp.int32, (rows, rows), 1)
    flip = jnp.where(row + column == rows - 1, 1.0, 0.0).astype(jnp.bfloat16)
    flipped = jnp.dot(flip, taps_ref[...], preferred_element_type=jnp.float32)
    flipped_t = flipped.T.astype(jnp.bfloat16)
    mirror = jnp.where(
        (row // GROUP == column // GROUP) & (row % GROUP + column % GROUP == GROUP - 1), 1.0, 0.0
    ).astype(jnp.bfloat16)
    value_t = jnp.concatenate(
        [
            lax.dot_general(
                mirror, value_ref[:, at : at + rows], NT, preferred_element_type=jnp.float32
            )
            for at in range(0, value_ref.shape[1], rows)
        ],
        axis=0,
    ).astype(jnp.bfloat16)
    for peer in range(peers):
        payload_ref[peer, :part, :] = value_t[peer * part : (peer + 1) * part]
        payload_ref[peer, part:, :] = flipped_t[peer * part : (peer + 1) * part]
    gate_t_ref[...] = gate_ref[...].astype(jnp.float32).T.astype(jnp.bfloat16)


def turned(value, filter_taps, gate_rows, peers):
    rows, channels = value.shape
    return pl.pallas_call(
        turn_kernel,
        out_shape=[
            jax.ShapeDtypeStruct((peers, 2 * channels // peers, rows), jnp.bfloat16),
            jax.ShapeDtypeStruct((channels, rows), jnp.bfloat16),
        ],
        compiler_params=pltpu.CompilerParams(vmem_limit_bytes=8 * 2**20),
    )(value, filter_taps, gate_rows)


def conv_kernel(payload_ref, place_ref, out_ref, value_ref, taps_ref, packed_ref):
    blocks, both, lanes = payload_ref.shape
    channels = both // 2
    length = blocks * lanes
    outer = lanes // SHIFTS
    tail = jnp.zeros((GROUP, lanes), jnp.float32)
    sides = SHIFTS * GROUP // lanes
    slot = lax.broadcasted_iota(jnp.int32, (GROUP, lanes), 1) % GROUP
    for group in range(channels // GROUP):
        first = group * GROUP
        padded = jnp.concatenate(
            [
                payload_ref[q, first : first + GROUP, :].astype(jnp.float32)
                for q in range(blocks)
            ]
            + [tail],
            axis=1,
        )
        for shift in range(SHIFTS):
            moved = pltpu.roll(padded, shift, 1) if shift else padded
            value_ref[group, shift * GROUP : (shift + 1) * GROUP, :] = moved[:, :length].astype(
                jnp.bfloat16
            )
        padded = jnp.concatenate(
            [
                payload_ref[blocks - 1 - q, channels + first : channels + first + GROUP, :].astype(
                    jnp.float32
                )
                for q in range(blocks)
            ]
            + [tail],
            axis=1,
        )
        for k in range(outer):
            left = SHIFTS * (outer - 1 - k)
            moved = pltpu.roll(padded, length + lanes - left, 1) if left else padded
            taps_ref[group, k * GROUP : (k + 1) * GROUP, :length] = moved[:, :length].astype(
                jnp.bfloat16
            )
        taps_ref[group, :, length:] = jnp.zeros((outer * GROUP, lanes), jnp.bfloat16)
        for pair in range(blocks // 2):
            span = 2 * lanes * (pair + 1)
            even = (blocks - 1 - 2 * pair) * lanes
            odd = even - lanes
            left_side = jnp.concatenate(
                [
                    taps_ref[group, :, even : even + span],
                    taps_ref[group, :, odd : odd + span],
                ],
                axis=0,
            )
            mixed = lax.dot_general(
                left_side, value_ref[group, :, :span], NT, preferred_element_type=jnp.float32
            )
            for half in range(2):
                for side in range(sides):
                    packed = None
                    for k in range(outer):
                        at = (half * outer + k) * GROUP
                        tile = mixed[at : at + GROUP, side * lanes : (side + 1) * lanes]
                        tile = pltpu.roll(tile, k + 1, 1, stride=1, stride_axis=0)
                        packed = tile if k == 0 else jnp.where(slot == k, tile, packed)
                    at = (group * blocks + 2 * pair + half) * GROUP
                    packed_ref[at : at + GROUP, side * lanes : (side + 1) * lanes] = packed.astype(
                        jnp.bfloat16
                    )
    result = jnp.dot(packed_ref[...], place_ref[...], preferred_element_type=jnp.float32)
    result = result.astype(jnp.bfloat16)
    for group in range(channels // GROUP):
        for block in range(blocks):
            at = (group * blocks + block) * GROUP
            out_ref[block, group * GROUP : (group + 1) * GROUP, :] = result[at : at + GROUP]


def placement(lanes):
    per_side = lanes // GROUP
    side, place, slot, t = np.ix_(
        range(SHIFTS // per_side), range(per_side), range(GROUP), range(lanes)
    )
    r = side * per_side + (place - 1) % per_side
    hit = t == SHIFTS * slot + SHIFTS - 1 - r
    return jnp.asarray(hit.reshape(SHIFTS * GROUP, lanes), jnp.bfloat16)


def convolve(payload):
    blocks, both, lanes = payload.shape
    channels = both // 2
    groups = channels // GROUP
    outer = lanes // SHIFTS
    return pl.pallas_call(
        conv_kernel,
        out_shape=jax.ShapeDtypeStruct((blocks, channels, lanes), jnp.bfloat16),
        scratch_shapes=[
            pltpu.VMEM((groups, SHIFTS * GROUP, blocks * lanes), jnp.bfloat16),
            pltpu.VMEM((groups, outer * GROUP, (blocks + 1) * lanes), jnp.bfloat16),
            pltpu.VMEM((groups * blocks * GROUP, SHIFTS * GROUP), jnp.bfloat16),
        ],
        cost_estimate=pl.CostEstimate(
            flops=2 * channels * GROUP * (blocks * lanes) ** 2,
            bytes_accessed=6 * channels * blocks * lanes,
            transcendentals=0,
        ),
        compiler_params=pltpu.CompilerParams(vmem_limit_bytes=24 * 2**20),
    )(payload, placement(lanes))


def gate_kernel(conv_ref, gate_ref, out_ref):
    out_ref[...] = (
        conv_ref[...].astype(jnp.float32) * gate_ref[...].astype(jnp.float32)
    ).astype(out_ref.dtype)


def gated(conv_t, gate_t):
    return pl.pallas_call(
        gate_kernel,
        out_shape=jax.ShapeDtypeStruct(conv_t.shape, jnp.bfloat16),
        compiler_params=pltpu.CompilerParams(vmem_limit_bytes=4 * 2**20),
    )(conv_t, gate_t)


def project_kernel(far, own_ref, other_ref, own_weight_ref, other_weight_ref, out_ref):
    features = out_ref.shape[1]
    rank = lax.axis_index("ch") ^ (2 if far else 0)
    span = pl.ds(pl.multiple_of(rank * features, features), features)
    total = lax.dot_general(
        own_ref[...], own_weight_ref[:, span], TN, preferred_element_type=jnp.float32
    )
    total += lax.dot_general(
        other_ref[...], other_weight_ref[:, span], TN, preferred_element_type=jnp.float32
    )
    out_ref[...] = total.astype(out_ref.dtype)


def project(own, other, own_weight, other_weight, features, far, dtype):
    return pl.pallas_call(
        functools.partial(project_kernel, far),
        out_shape=jax.ShapeDtypeStruct((own.shape[1], features), dtype),
        compiler_params=pltpu.CompilerParams(vmem_limit_bytes=24 * 2**20),
    )(own, other, own_weight, other_weight)


def by_blocks(tokens, value_weight, gate_rows, filter_taps, out_weight):
    peers = lax.axis_size("ctx")
    ranks = lax.axis_size("ch")
    features = out_weight.shape[1] // ranks
    near = [(i, i ^ 1) for i in range(ranks)]
    far = [(i, i ^ 2) for i in range(ranks)]
    value = jnp.dot(tokens, value_weight, preferred_element_type=jnp.float32).astype(
        jnp.bfloat16
    )
    payload, gate_t = turned(value, filter_taps, gate_rows, peers)
    other_weight = lax.ppermute(out_weight, "ch", near)
    payload = lax.all_to_all(payload, "ctx", split_axis=0, concat_axis=0, tiled=True)
    conv = convolve(payload)
    conv = lax.all_to_all(conv, "ctx", split_axis=0, concat_axis=0, tiled=True)
    own = gated(conv.reshape(gate_t.shape), gate_t)
    other = lax.ppermute(own, "ch", near)
    sent = project(own, other, out_weight, other_weight, features, True, jnp.bfloat16)
    arrived = lax.ppermute(sent, "ch", far)
    kept = project(own, other, out_weight, other_weight, features, False, jnp.float32)
    return (kept + arrived.astype(jnp.float32)).astype(jnp.bfloat16)


def fits_blocks(tokens, value_weight, peers, ranks):
    rows, channels = tokens.shape[0], value_weight.shape[1]
    return (
        rows == LANES
        and ranks == 4
        and peers % 2 == 0
        and peers <= 16
        and channels % (peers * GROUP) == 0
    )


def on_device(tokens, value_weight, gate_rows, filter_taps, out_weight):
    peers, ranks = lax.axis_size("ctx"), lax.axis_size("ch")
    if fits_blocks(tokens, value_weight, peers, ranks):
        return by_blocks(tokens, value_weight, gate_rows, filter_taps, out_weight)
    return by_transform(tokens, value_weight, gate_rows, filter_taps, out_weight)


def solution(mesh):
    placed = (P("ctx", None), P(None, "ch"), P("ctx", "ch"), P("ctx", "ch"), P("ch", None))
    return jax.shard_map(
        on_device, mesh=mesh, in_specs=placed, out_specs=P("ctx", "ch"), check_vma=False
    )
```

```python
import functools
import math

import jax
import jax.numpy as jnp
import numpy as np
from jax import lax
from jax.experimental import pallas as pl
from jax.experimental.pallas import tpu as pltpu
from jax.sharding import PartitionSpec as P

HIGHEST = lax.Precision.HIGHEST


def column_tables(half_rows, peer_count):
    rows_full = 2 * half_rows
    length = rows_full * peer_count
    outer_freq = jnp.arange(rows_full, dtype=jnp.int32)[:, None]
    outer_pos = jnp.arange(half_rows, dtype=jnp.int32)[None, :]
    first_angle = (
        -2.0 * math.pi / rows_full * (outer_freq * outer_pos % rows_full).astype(jnp.float32)
    )
    inner_pos = jnp.arange(peer_count, dtype=jnp.int32)[None, :]
    twist_angle = -2.0 * math.pi / length * (outer_freq * inner_pos % length).astype(jnp.float32)
    inner_index = jnp.arange(peer_count, dtype=jnp.int32)
    second_angle = (
        -2.0
        * math.pi
        / peer_count
        * (inner_index[:, None] * inner_index[None, :] % peer_count).astype(jnp.float32)
    )
    return (
        jnp.cos(first_angle),
        jnp.sin(first_angle),
        jnp.cos(twist_angle),
        jnp.sin(twist_angle),
        jnp.cos(second_angle),
        jnp.sin(second_angle),
    )


def column_spectrum(signal, tables):
    first_cos, first_sin, twist_cos, twist_sin, second_cos, second_sin = tables
    section_real = jnp.einsum("kn,nbc->ckb", first_cos, signal, precision=HIGHEST)
    section_imag = jnp.einsum("kn,nbc->ckb", first_sin, signal, precision=HIGHEST)
    turned_real = section_real * twist_cos - section_imag * twist_sin
    turned_imag = section_real * twist_sin + section_imag * twist_cos

    def apply_second(table_part, operand):
        return jnp.einsum("ckb,bj->ckj", operand, table_part, precision=HIGHEST)

    spec_real = apply_second(second_cos, turned_real) - apply_second(second_sin, turned_imag)
    spec_imag = apply_second(second_sin, turned_real) + apply_second(second_cos, turned_imag)
    return (spec_real, spec_imag)


def column_inverse(spec_real, spec_imag, tables):
    first_cos, first_sin, twist_cos, twist_sin, second_cos, second_sin = tables

    def apply_second(table_part, operand):
        return jnp.einsum("ckj,bj->ckb", operand, table_part, precision=HIGHEST)

    back_real = apply_second(second_cos, spec_real) + apply_second(second_sin, spec_imag)
    back_imag = apply_second(second_cos, spec_imag) - apply_second(second_sin, spec_real)
    turned_real = back_real * twist_cos + back_imag * twist_sin
    turned_imag = back_imag * twist_cos - back_real * twist_sin
    return jnp.einsum("kn,ckb->nbc", first_cos, turned_real, precision=HIGHEST) + jnp.einsum(
        "kn,ckb->nbc", first_sin, turned_imag, precision=HIGHEST
    )


def by_transform(tokens, value_weight, gate_rows, filter_taps, out_weight):
    local_rows = tokens.shape[0]
    peer_count = lax.axis_size("ctx")
    length = peer_count * local_rows
    value_rows = jnp.dot(tokens, value_weight, preferred_element_type=jnp.float32).astype(
        jnp.bfloat16
    )
    value_columns = lax.all_to_all(value_rows, "ctx", split_axis=1, concat_axis=0, tiled=True)
    tap_columns = lax.all_to_all(filter_taps, "ctx", split_axis=1, concat_axis=0, tiled=True)
    channels_here = value_columns.shape[1]
    tables = column_tables(local_rows, peer_count)
    value_signal = value_columns.astype(jnp.float32).reshape(local_rows, peer_count, channels_here)
    tap_signal = tap_columns.astype(jnp.float32).reshape(local_rows, peer_count, channels_here)
    value_real, value_imag = column_spectrum(value_signal, tables)
    tap_real, tap_imag = column_spectrum(tap_signal, tables)
    product_real = value_real * tap_real - value_imag * tap_imag
    product_imag = value_real * tap_imag + value_imag * tap_real
    restored = column_inverse(product_real, product_imag, tables) / (2.0 * length)
    restored = restored.reshape(length, channels_here).astype(jnp.bfloat16)
    convolved = lax.all_to_all(restored, "ctx", split_axis=0, concat_axis=1, tiled=True)
    gated_rows = (convolved.astype(jnp.float32) * gate_rows.astype(jnp.float32)).astype(
        jnp.bfloat16
    )
    partial_sum = jnp.dot(gated_rows, out_weight, preferred_element_type=jnp.float32)
    own_sum = lax.psum_scatter(
        partial_sum.astype(jnp.bfloat16), "ch", scatter_dimension=1, tiled=True
    )
    return own_sum


LANES = 128
SHIFTS = 16
GROUP = 16
NT = (((1,), (1,)), ((), ()))
TN = (((0,), (0,)), ((), ()))


def turn_kernel(value_ref, taps_ref, gate_ref, payload_ref, gate_t_ref):
    peers, both, rows = payload_ref.shape
    part = both // 2
    row = lax.broadcasted_iota(jnp.int32, (rows, rows), 0)
    column = lax.broadcasted_iota(jnp.int32, (rows, rows), 1)
    flip = jnp.where(row + column == rows - 1, 1.0, 0.0).astype(jnp.bfloat16)
    flipped = jnp.dot(flip, taps_ref[...], preferred_element_type=jnp.float32)
    flipped_t = flipped.T.astype(jnp.bfloat16)
    mirror = jnp.where(
        (row // GROUP == column // GROUP) & (row % GROUP + column % GROUP == GROUP - 1), 1.0, 0.0
    ).astype(jnp.bfloat16)
    value_t = jnp.concatenate(
        [
            lax.dot_general(
                mirror, value_ref[:, at : at + rows], NT, preferred_element_type=jnp.float32
            )
            for at in range(0, value_ref.shape[1], rows)
        ],
        axis=0,
    ).astype(jnp.bfloat16)
    for peer in range(peers):
        payload_ref[peer, :part, :] = value_t[peer * part : (peer + 1) * part]
        payload_ref[peer, part:, :] = flipped_t[peer * part : (peer + 1) * part]
    gate_t_ref[...] = gate_ref[...].astype(jnp.float32).T.astype(jnp.bfloat16)


def turned(value, filter_taps, gate_rows, peers):
    rows, channels = value.shape
    return pl.pallas_call(
        turn_kernel,
        out_shape=[
            jax.ShapeDtypeStruct((peers, 2 * channels // peers, rows), jnp.bfloat16),
            jax.ShapeDtypeStruct((channels, rows), jnp.bfloat16),
        ],
        compiler_params=pltpu.CompilerParams(vmem_limit_bytes=8 * 2**20),
    )(value, filter_taps, gate_rows)


def conv_kernel(payload_ref, place_ref, out_ref, value_ref, taps_ref, packed_ref):
    blocks, both, lanes = payload_ref.shape
    channels = both // 2
    length = blocks * lanes
    outer = lanes // SHIFTS
    tail = jnp.zeros((GROUP, lanes), jnp.float32)
    sides = SHIFTS * GROUP // lanes
    slot = lax.broadcasted_iota(jnp.int32, (GROUP, lanes), 1) % GROUP
    def build(group):
        first = group * GROUP
        padded = jnp.concatenate(
            [
                payload_ref[q, first : first + GROUP, :].astype(jnp.float32)
                for q in range(blocks)
            ]
            + [tail],
            axis=1,
        )
        for shift in range(SHIFTS):
            moved = pltpu.roll(padded, shift, 1) if shift else padded
            value_ref[group, shift * GROUP : (shift + 1) * GROUP, :] = moved[:, :length].astype(
                jnp.bfloat16
            )
        padded = jnp.concatenate(
            [
                payload_ref[blocks - 1 - q, channels + first : channels + first + GROUP, :].astype(
                    jnp.float32
                )
                for q in range(blocks)
            ]
            + [tail],
            axis=1,
        )
        for k in range(outer):
            left = SHIFTS * (outer - 1 - k)
            moved = pltpu.roll(padded, length + lanes - left, 1) if left else padded
            taps_ref[group, k * GROUP : (k + 1) * GROUP, :length] = moved[:, :length].astype(
                jnp.bfloat16
            )
        taps_ref[group, :, length:] = jnp.zeros((outer * GROUP, lanes), jnp.bfloat16)

    def mix(group):
        for pair in range(blocks // 2):
            span = 2 * lanes * (pair + 1)
            even = (blocks - 1 - 2 * pair) * lanes
            odd = even - lanes
            left_side = jnp.concatenate(
                [
                    taps_ref[group, :, even : even + span],
                    taps_ref[group, :, odd : odd + span],
                ],
                axis=0,
            )
            mixed = lax.dot_general(
                left_side, value_ref[group, :, :span], NT, preferred_element_type=jnp.float32
            )
            for half in range(2):
                for side in range(sides):
                    packed = None
                    for k in range(outer):
                        at = (half * outer + k) * GROUP
                        tile = mixed[at : at + GROUP, side * lanes : (side + 1) * lanes]
                        tile = pltpu.roll(tile, k + 1, 1, stride=1, stride_axis=0)
                        packed = tile if k == 0 else jnp.where(slot == k, tile, packed)
                    at = (group * blocks + 2 * pair + half) * GROUP
                    packed_ref[at : at + GROUP, side * lanes : (side + 1) * lanes] = packed.astype(
                        jnp.bfloat16
                    )

    groups = channels // GROUP
    build(0)
    for group in range(groups):
        if group + 1 < groups:
            build(group + 1)
        mix(group)
    result = jnp.dot(packed_ref[...], place_ref[...], preferred_element_type=jnp.float32)
    result = result.astype(jnp.bfloat16)
    for group in range(channels // GROUP):
        for block in range(blocks):
            at = (group * blocks + block) * GROUP
            out_ref[block, group * GROUP : (group + 1) * GROUP, :] = result[at : at + GROUP]


def placement(lanes):
    per_side = lanes // GROUP
    side, place, slot, t = np.ix_(
        range(SHIFTS // per_side), range(per_side), range(GROUP), range(lanes)
    )
    r = side * per_side + (place - 1) % per_side
    hit = t == SHIFTS * slot + SHIFTS - 1 - r
    return jnp.asarray(hit.reshape(SHIFTS * GROUP, lanes), jnp.bfloat16)


def convolve(payload):
    blocks, both, lanes = payload.shape
    channels = both // 2
    groups = channels // GROUP
    outer = lanes // SHIFTS
    return pl.pallas_call(
        conv_kernel,
        out_shape=jax.ShapeDtypeStruct((blocks, channels, lanes), jnp.bfloat16),
        scratch_shapes=[
            pltpu.VMEM((groups, SHIFTS * GROUP, blocks * lanes), jnp.bfloat16),
            pltpu.VMEM((groups, outer * GROUP, (blocks + 1) * lanes), jnp.bfloat16),
            pltpu.VMEM((groups * blocks * GROUP, SHIFTS * GROUP), jnp.bfloat16),
        ],
        cost_estimate=pl.CostEstimate(
            flops=2 * channels * GROUP * (blocks * lanes) ** 2,
            bytes_accessed=6 * channels * blocks * lanes,
            transcendentals=0,
        ),
        compiler_params=pltpu.CompilerParams(vmem_limit_bytes=24 * 2**20),
    )(payload, placement(lanes))


def gate_kernel(conv_ref, gate_ref, out_ref):
    out_ref[...] = (
        conv_ref[...].astype(jnp.float32) * gate_ref[...].astype(jnp.float32)
    ).astype(out_ref.dtype)


def gated(conv_t, gate_t):
    return pl.pallas_call(
        gate_kernel,
        out_shape=jax.ShapeDtypeStruct(conv_t.shape, jnp.bfloat16),
        compiler_params=pltpu.CompilerParams(vmem_limit_bytes=4 * 2**20),
    )(conv_t, gate_t)


def project_kernel(flip, own_ref, weight_ref, out_ref):
    features = out_ref.shape[1]
    at = (lax.axis_index("ch") ^ flip) * features
    out_ref[...] = lax.dot_general(
        own_ref[...],
        weight_ref[:, pl.ds(pl.multiple_of(at, features), features)],
        TN,
        preferred_element_type=jnp.float32,
    ).astype(out_ref.dtype)


def project(own, weight, features, flip, dtype):
    depth, rows = own.shape
    return pl.pallas_call(
        functools.partial(project_kernel, flip),
        out_shape=jax.ShapeDtypeStruct((rows, features), dtype),
        cost_estimate=pl.CostEstimate(
            flops=2 * rows * depth * features,
            bytes_accessed=2 * depth * features + 4 * rows * features,
            transcendentals=0,
        ),
        compiler_params=pltpu.CompilerParams(vmem_limit_bytes=24 * 2**20),
    )(own, weight)


def add_kernel(first_ref, second_ref, out_ref):
    out_ref[...] = (first_ref[...] + second_ref[...].astype(jnp.float32)).astype(out_ref.dtype)


def added(first, second):
    return pl.pallas_call(
        add_kernel,
        out_shape=jax.ShapeDtypeStruct(first.shape, jnp.bfloat16),
        compiler_params=pltpu.CompilerParams(vmem_limit_bytes=8 * 2**20),
    )(first, second)


def by_blocks(tokens, value_weight, gate_rows, filter_taps, out_weight):
    peers = lax.axis_size("ctx")
    ranks = lax.axis_size("ch")
    features = out_weight.shape[1] // ranks
    near = [(i, i ^ 1) for i in range(ranks)]
    far = [(i, i ^ 2) for i in range(ranks)]
    value = jnp.dot(tokens, value_weight, preferred_element_type=jnp.float32).astype(
        jnp.bfloat16
    )
    payload, gate_t = turned(value, filter_taps, gate_rows, peers)
    payload = lax.all_to_all(payload, "ctx", split_axis=0, concat_axis=0, tiled=True)
    conv = convolve(payload)
    conv = lax.all_to_all(conv, "ctx", split_axis=0, concat_axis=0, tiled=True)
    own = gated(conv.reshape(gate_t.shape), gate_t)
    far_near = lax.ppermute(project(own, out_weight, features, 3, jnp.bfloat16), "ch", near)
    far_own = project(own, out_weight, features, 2, jnp.float32)
    sent = added(far_own, far_near)
    arrived = lax.ppermute(sent, "ch", far)
    kept_near = lax.ppermute(project(own, out_weight, features, 1, jnp.bfloat16), "ch", near)
    kept = project(own, out_weight, features, 0, jnp.float32)
    return (
        kept + kept_near.astype(jnp.float32) + arrived.astype(jnp.float32)
    ).astype(jnp.bfloat16)


def fits_blocks(tokens, value_weight, peers, ranks):
    rows, channels = tokens.shape[0], value_weight.shape[1]
    return (
        rows == LANES
        and ranks == 4
        and peers % 2 == 0
        and peers <= 16
        and channels % (peers * GROUP) == 0
    )


def on_device(tokens, value_weight, gate_rows, filter_taps, out_weight):
    peers, ranks = lax.axis_size("ctx"), lax.axis_size("ch")
    if fits_blocks(tokens, value_weight, peers, ranks):
        return by_blocks(tokens, value_weight, gate_rows, filter_taps, out_weight)
    return by_transform(tokens, value_weight, gate_rows, filter_taps, out_weight)


def solution(mesh):
    placed = (P("ctx", None), P(None, "ch"), P("ctx", "ch"), P("ctx", "ch"), P("ch", None))
    return jax.shard_map(
        on_device, mesh=mesh, in_specs=placed, out_specs=P("ctx", "ch"), check_vma=False
    )
```

```python
import functools
import math

import jax
import jax.numpy as jnp
import numpy as np
from jax import lax
from jax.experimental import pallas as pl
from jax.experimental.pallas import tpu as pltpu
from jax.sharding import PartitionSpec as P

HIGHEST = lax.Precision.HIGHEST


def column_tables(half_rows, peer_count):
    rows_full = 2 * half_rows
    length = rows_full * peer_count
    outer_freq = jnp.arange(rows_full, dtype=jnp.int32)[:, None]
    outer_pos = jnp.arange(half_rows, dtype=jnp.int32)[None, :]
    first_angle = (
        -2.0 * math.pi / rows_full * (outer_freq * outer_pos % rows_full).astype(jnp.float32)
    )
    inner_pos = jnp.arange(peer_count, dtype=jnp.int32)[None, :]
    twist_angle = -2.0 * math.pi / length * (outer_freq * inner_pos % length).astype(jnp.float32)
    inner_index = jnp.arange(peer_count, dtype=jnp.int32)
    second_angle = (
        -2.0
        * math.pi
        / peer_count
        * (inner_index[:, None] * inner_index[None, :] % peer_count).astype(jnp.float32)
    )
    return (
        jnp.cos(first_angle),
        jnp.sin(first_angle),
        jnp.cos(twist_angle),
        jnp.sin(twist_angle),
        jnp.cos(second_angle),
        jnp.sin(second_angle),
    )


def column_spectrum(signal, tables):
    first_cos, first_sin, twist_cos, twist_sin, second_cos, second_sin = tables
    section_real = jnp.einsum("kn,nbc->ckb", first_cos, signal, precision=HIGHEST)
    section_imag = jnp.einsum("kn,nbc->ckb", first_sin, signal, precision=HIGHEST)
    turned_real = section_real * twist_cos - section_imag * twist_sin
    turned_imag = section_real * twist_sin + section_imag * twist_cos

    def apply_second(table_part, operand):
        return jnp.einsum("ckb,bj->ckj", operand, table_part, precision=HIGHEST)

    spec_real = apply_second(second_cos, turned_real) - apply_second(second_sin, turned_imag)
    spec_imag = apply_second(second_sin, turned_real) + apply_second(second_cos, turned_imag)
    return (spec_real, spec_imag)


def column_inverse(spec_real, spec_imag, tables):
    first_cos, first_sin, twist_cos, twist_sin, second_cos, second_sin = tables

    def apply_second(table_part, operand):
        return jnp.einsum("ckj,bj->ckb", operand, table_part, precision=HIGHEST)

    back_real = apply_second(second_cos, spec_real) + apply_second(second_sin, spec_imag)
    back_imag = apply_second(second_cos, spec_imag) - apply_second(second_sin, spec_real)
    turned_real = back_real * twist_cos + back_imag * twist_sin
    turned_imag = back_imag * twist_cos - back_real * twist_sin
    return jnp.einsum("kn,ckb->nbc", first_cos, turned_real, precision=HIGHEST) + jnp.einsum(
        "kn,ckb->nbc", first_sin, turned_imag, precision=HIGHEST
    )


def by_transform(tokens, value_weight, gate_rows, filter_taps, out_weight):
    local_rows = tokens.shape[0]
    peer_count = lax.axis_size("ctx")
    length = peer_count * local_rows
    value_rows = jnp.dot(tokens, value_weight, preferred_element_type=jnp.float32).astype(
        jnp.bfloat16
    )
    value_columns = lax.all_to_all(value_rows, "ctx", split_axis=1, concat_axis=0, tiled=True)
    tap_columns = lax.all_to_all(filter_taps, "ctx", split_axis=1, concat_axis=0, tiled=True)
    channels_here = value_columns.shape[1]
    tables = column_tables(local_rows, peer_count)
    value_signal = value_columns.astype(jnp.float32).reshape(local_rows, peer_count, channels_here)
    tap_signal = tap_columns.astype(jnp.float32).reshape(local_rows, peer_count, channels_here)
    value_real, value_imag = column_spectrum(value_signal, tables)
    tap_real, tap_imag = column_spectrum(tap_signal, tables)
    product_real = value_real * tap_real - value_imag * tap_imag
    product_imag = value_real * tap_imag + value_imag * tap_real
    restored = column_inverse(product_real, product_imag, tables) / (2.0 * length)
    restored = restored.reshape(length, channels_here).astype(jnp.bfloat16)
    convolved = lax.all_to_all(restored, "ctx", split_axis=0, concat_axis=1, tiled=True)
    gated_rows = (convolved.astype(jnp.float32) * gate_rows.astype(jnp.float32)).astype(
        jnp.bfloat16
    )
    partial_sum = jnp.dot(gated_rows, out_weight, preferred_element_type=jnp.float32)
    own_sum = lax.psum_scatter(
        partial_sum.astype(jnp.bfloat16), "ch", scatter_dimension=1, tiled=True
    )
    return own_sum


LANES = 128
SHIFTS = 16
GROUP = 16
AHEAD_FLOPS = 4 * 2**30
NT = (((1,), (1,)), ((), ()))
TN = (((0,), (0,)), ((), ()))


def orders_kernel(flip_ref, mirror_ref):
    rows = flip_ref.shape[0]
    row = lax.broadcasted_iota(jnp.int32, (rows, rows), 0)
    column = lax.broadcasted_iota(jnp.int32, (rows, rows), 1)
    flip_ref[...] = jnp.where(row + column == rows - 1, 1.0, 0.0).astype(jnp.bfloat16)
    mirror_ref[...] = jnp.where(
        (row // GROUP == column // GROUP) & (row % GROUP + column % GROUP == GROUP - 1), 1.0, 0.0
    ).astype(jnp.bfloat16)


def orders(rows):
    shape = jax.ShapeDtypeStruct((rows, rows), jnp.bfloat16)
    return pl.pallas_call(
        orders_kernel,
        out_shape=[shape, shape],
        cost_estimate=pl.CostEstimate(
            flops=AHEAD_FLOPS, bytes_accessed=4 * rows * rows, transcendentals=0
        ),
        compiler_params=pltpu.CompilerParams(vmem_limit_bytes=4 * 2**20),
    )()


def turn_kernel(flip_ref, mirror_ref, value_ref, taps_ref, gate_ref, payload_ref, gate_t_ref):
    peers, both, rows = payload_ref.shape
    part = both // 2
    flipped = jnp.dot(flip_ref[...], taps_ref[...], preferred_element_type=jnp.float32)
    flipped_t = flipped.T.astype(jnp.bfloat16)
    value_t = jnp.concatenate(
        [
            lax.dot_general(
                mirror_ref[...], value_ref[:, at : at + rows], NT, preferred_element_type=jnp.float32
            )
            for at in range(0, value_ref.shape[1], rows)
        ],
        axis=0,
    ).astype(jnp.bfloat16)
    for peer in range(peers):
        payload_ref[peer, :part, :] = value_t[peer * part : (peer + 1) * part]
        payload_ref[peer, part:, :] = flipped_t[peer * part : (peer + 1) * part]
    gate_t_ref[...] = gate_ref[...].astype(jnp.float32).T.astype(jnp.bfloat16)


def turned(flip, mirror, value, filter_taps, gate_rows, peers):
    rows, channels = value.shape
    return pl.pallas_call(
        turn_kernel,
        out_shape=[
            jax.ShapeDtypeStruct((peers, 2 * channels // peers, rows), jnp.bfloat16),
            jax.ShapeDtypeStruct((channels, rows), jnp.bfloat16),
        ],
        compiler_params=pltpu.CompilerParams(vmem_limit_bytes=8 * 2**20),
    )(flip, mirror, value, filter_taps, gate_rows)


def conv_kernel(payload_ref, place_ref, out_ref, value_ref, taps_ref, packed_ref):
    blocks, both, lanes = payload_ref.shape
    channels = both // 2
    length = blocks * lanes
    outer = lanes // SHIFTS
    tail = jnp.zeros((GROUP, lanes), jnp.float32)
    sides = SHIFTS * GROUP // lanes
    slot = lax.broadcasted_iota(jnp.int32, (GROUP, lanes), 1) % GROUP
    def build(group):
        first = group * GROUP
        padded = jnp.concatenate(
            [
                payload_ref[q, first : first + GROUP, :].astype(jnp.float32)
                for q in range(blocks)
            ]
            + [tail],
            axis=1,
        )
        for shift in range(SHIFTS):
            moved = pltpu.roll(padded, shift, 1) if shift else padded
            value_ref[group, shift * GROUP : (shift + 1) * GROUP, :] = moved[:, :length].astype(
                jnp.bfloat16
            )
        padded = jnp.concatenate(
            [
                payload_ref[blocks - 1 - q, channels + first : channels + first + GROUP, :].astype(
                    jnp.float32
                )
                for q in range(blocks)
            ]
            + [tail],
            axis=1,
        )
        for k in range(outer):
            left = SHIFTS * (outer - 1 - k)
            moved = pltpu.roll(padded, length + lanes - left, 1) if left else padded
            taps_ref[group, k * GROUP : (k + 1) * GROUP, :length] = moved[:, :length].astype(
                jnp.bfloat16
            )
        taps_ref[group, :, length:] = jnp.zeros((outer * GROUP, lanes), jnp.bfloat16)

    def mix(group):
        for pair in range(blocks // 2):
            span = 2 * lanes * (pair + 1)
            even = (blocks - 1 - 2 * pair) * lanes
            odd = even - lanes
            left_side = jnp.concatenate(
                [
                    taps_ref[group, :, even : even + span],
                    taps_ref[group, :, odd : odd + span],
                ],
                axis=0,
            )
            mixed = lax.dot_general(
                left_side, value_ref[group, :, :span], NT, preferred_element_type=jnp.float32
            )
            for half in range(2):
                for side in range(sides):
                    packed = None
                    for k in range(outer):
                        at = (half * outer + k) * GROUP
                        tile = mixed[at : at + GROUP, side * lanes : (side + 1) * lanes]
                        tile = pltpu.roll(tile, k + 1, 1, stride=1, stride_axis=0)
                        packed = tile if k == 0 else jnp.where(slot == k, tile, packed)
                    at = (group * blocks + 2 * pair + half) * GROUP
                    packed_ref[at : at + GROUP, side * lanes : (side + 1) * lanes] = packed.astype(
                        jnp.bfloat16
                    )

    groups = channels // GROUP
    build(0)
    for group in range(groups):
        if group + 1 < groups:
            build(group + 1)
        mix(group)
    result = jnp.dot(packed_ref[...], place_ref[...], preferred_element_type=jnp.float32)
    result = result.astype(jnp.bfloat16)
    for group in range(channels // GROUP):
        for block in range(blocks):
            at = (group * blocks + block) * GROUP
            out_ref[block, group * GROUP : (group + 1) * GROUP, :] = result[at : at + GROUP]


def placement(lanes):
    per_side = lanes // GROUP
    side, place, slot, t = np.ix_(
        range(SHIFTS // per_side), range(per_side), range(GROUP), range(lanes)
    )
    r = side * per_side + (place - 1) % per_side
    hit = t == SHIFTS * slot + SHIFTS - 1 - r
    return jnp.asarray(hit.reshape(SHIFTS * GROUP, lanes), jnp.bfloat16)


def convolve(payload):
    blocks, both, lanes = payload.shape
    channels = both // 2
    groups = channels // GROUP
    outer = lanes // SHIFTS
    return pl.pallas_call(
        conv_kernel,
        out_shape=jax.ShapeDtypeStruct((blocks, channels, lanes), jnp.bfloat16),
        scratch_shapes=[
            pltpu.VMEM((groups, SHIFTS * GROUP, blocks * lanes), jnp.bfloat16),
            pltpu.VMEM((groups, outer * GROUP, (blocks + 1) * lanes), jnp.bfloat16),
            pltpu.VMEM((groups * blocks * GROUP, SHIFTS * GROUP), jnp.bfloat16),
        ],
        cost_estimate=pl.CostEstimate(
            flops=2 * channels * GROUP * (blocks * lanes) ** 2,
            bytes_accessed=6 * channels * blocks * lanes,
            transcendentals=0,
        ),
        compiler_params=pltpu.CompilerParams(vmem_limit_bytes=24 * 2**20),
    )(payload, placement(lanes))


def gate_kernel(conv_ref, gate_ref, out_ref):
    out_ref[...] = (
        conv_ref[...].astype(jnp.float32) * gate_ref[...].astype(jnp.float32)
    ).astype(out_ref.dtype)


def gated(conv_t, gate_t):
    return pl.pallas_call(
        gate_kernel,
        out_shape=jax.ShapeDtypeStruct(conv_t.shape, jnp.bfloat16),
        compiler_params=pltpu.CompilerParams(vmem_limit_bytes=4 * 2**20),
    )(conv_t, gate_t)


def project_kernel(flip, own_ref, weight_ref, out_ref):
    features = out_ref.shape[1]
    at = (lax.axis_index("ch") ^ flip) * features
    out_ref[...] = lax.dot_general(
        own_ref[...],
        weight_ref[:, pl.ds(pl.multiple_of(at, features), features)],
        TN,
        preferred_element_type=jnp.float32,
    ).astype(out_ref.dtype)


def project(own, weight, features, flip, dtype):
    depth, rows = own.shape
    return pl.pallas_call(
        functools.partial(project_kernel, flip),
        out_shape=jax.ShapeDtypeStruct((rows, features), dtype),
        cost_estimate=pl.CostEstimate(
            flops=2 * rows * depth * features,
            bytes_accessed=2 * depth * features + 4 * rows * features,
            transcendentals=0,
        ),
        compiler_params=pltpu.CompilerParams(vmem_limit_bytes=24 * 2**20),
    )(own, weight)


def add_kernel(first_ref, second_ref, out_ref):
    out_ref[...] = (first_ref[...] + second_ref[...].astype(jnp.float32)).astype(out_ref.dtype)


def added(first, second):
    return pl.pallas_call(
        add_kernel,
        out_shape=jax.ShapeDtypeStruct(first.shape, jnp.bfloat16),
        compiler_params=pltpu.CompilerParams(vmem_limit_bytes=8 * 2**20),
    )(first, second)


def by_blocks(tokens, value_weight, gate_rows, filter_taps, out_weight):
    peers = lax.axis_size("ctx")
    ranks = lax.axis_size("ch")
    features = out_weight.shape[1] // ranks
    near = [(i, i ^ 1) for i in range(ranks)]
    far = [(i, i ^ 2) for i in range(ranks)]
    flip, mirror = orders(tokens.shape[0])
    flip, tokens, value_weight, filter_taps, gate_rows = lax.optimization_barrier(
        (flip, tokens, value_weight, filter_taps, gate_rows)
    )
    value = jnp.dot(tokens, value_weight, preferred_element_type=jnp.float32).astype(
        jnp.bfloat16
    )
    payload, gate_t = turned(flip, mirror, value, filter_taps, gate_rows, peers)
    payload = lax.all_to_all(payload, "ctx", split_axis=0, concat_axis=0, tiled=True)
    conv = convolve(payload)
    conv = lax.all_to_all(conv, "ctx", split_axis=0, concat_axis=0, tiled=True)
    own = gated(conv.reshape(gate_t.shape), gate_t)
    far_near = lax.ppermute(project(own, out_weight, features, 3, jnp.bfloat16), "ch", near)
    far_own = project(own, out_weight, features, 2, jnp.float32)
    sent = added(far_own, far_near)
    arrived = lax.ppermute(sent, "ch", far)
    kept_near = lax.ppermute(project(own, out_weight, features, 1, jnp.bfloat16), "ch", near)
    kept = project(own, out_weight, features, 0, jnp.float32)
    return (
        kept + kept_near.astype(jnp.float32) + arrived.astype(jnp.float32)
    ).astype(jnp.bfloat16)


def fits_blocks(tokens, value_weight, peers, ranks):
    rows, channels = tokens.shape[0], value_weight.shape[1]
    return (
        rows == LANES
        and ranks == 4
        and peers % 2 == 0
        and peers <= 16
        and channels % (peers * GROUP) == 0
    )


def on_device(tokens, value_weight, gate_rows, filter_taps, out_weight):
    peers, ranks = lax.axis_size("ctx"), lax.axis_size("ch")
    if fits_blocks(tokens, value_weight, peers, ranks):
        return by_blocks(tokens, value_weight, gate_rows, filter_taps, out_weight)
    return by_transform(tokens, value_weight, gate_rows, filter_taps, out_weight)


def solution(mesh):
    placed = (P("ctx", None), P(None, "ch"), P("ctx", "ch"), P("ctx", "ch"), P("ch", None))
    return jax.shard_map(
        on_device, mesh=mesh, in_specs=placed, out_specs=P("ctx", "ch"), check_vma=False
    )
```

```python
import functools
import math

import jax
import jax.numpy as jnp
import numpy as np
from jax import lax
from jax.experimental import pallas as pl
from jax.experimental.pallas import tpu as pltpu
from jax.sharding import PartitionSpec as P

HIGHEST = lax.Precision.HIGHEST


def column_tables(half_rows, peer_count):
    rows_full = 2 * half_rows
    length = rows_full * peer_count
    outer_freq = jnp.arange(rows_full, dtype=jnp.int32)[:, None]
    outer_pos = jnp.arange(half_rows, dtype=jnp.int32)[None, :]
    first_angle = (
        -2.0 * math.pi / rows_full * (outer_freq * outer_pos % rows_full).astype(jnp.float32)
    )
    inner_pos = jnp.arange(peer_count, dtype=jnp.int32)[None, :]
    twist_angle = -2.0 * math.pi / length * (outer_freq * inner_pos % length).astype(jnp.float32)
    inner_index = jnp.arange(peer_count, dtype=jnp.int32)
    second_angle = (
        -2.0
        * math.pi
        / peer_count
        * (inner_index[:, None] * inner_index[None, :] % peer_count).astype(jnp.float32)
    )
    return (
        jnp.cos(first_angle),
        jnp.sin(first_angle),
        jnp.cos(twist_angle),
        jnp.sin(twist_angle),
        jnp.cos(second_angle),
        jnp.sin(second_angle),
    )


def column_spectrum(signal, tables):
    first_cos, first_sin, twist_cos, twist_sin, second_cos, second_sin = tables
    section_real = jnp.einsum("kn,nbc->ckb", first_cos, signal, precision=HIGHEST)
    section_imag = jnp.einsum("kn,nbc->ckb", first_sin, signal, precision=HIGHEST)
    turned_real = section_real * twist_cos - section_imag * twist_sin
    turned_imag = section_real * twist_sin + section_imag * twist_cos

    def apply_second(table_part, operand):
        return jnp.einsum("ckb,bj->ckj", operand, table_part, precision=HIGHEST)

    spec_real = apply_second(second_cos, turned_real) - apply_second(second_sin, turned_imag)
    spec_imag = apply_second(second_sin, turned_real) + apply_second(second_cos, turned_imag)
    return (spec_real, spec_imag)


def column_inverse(spec_real, spec_imag, tables):
    first_cos, first_sin, twist_cos, twist_sin, second_cos, second_sin = tables

    def apply_second(table_part, operand):
        return jnp.einsum("ckj,bj->ckb", operand, table_part, precision=HIGHEST)

    back_real = apply_second(second_cos, spec_real) + apply_second(second_sin, spec_imag)
    back_imag = apply_second(second_cos, spec_imag) - apply_second(second_sin, spec_real)
    turned_real = back_real * twist_cos + back_imag * twist_sin
    turned_imag = back_imag * twist_cos - back_real * twist_sin
    return jnp.einsum("kn,ckb->nbc", first_cos, turned_real, precision=HIGHEST) + jnp.einsum(
        "kn,ckb->nbc", first_sin, turned_imag, precision=HIGHEST
    )


def by_transform(tokens, value_weight, gate_rows, filter_taps, out_weight):
    local_rows = tokens.shape[0]
    peer_count = lax.axis_size("ctx")
    length = peer_count * local_rows
    value_rows = jnp.dot(tokens, value_weight, preferred_element_type=jnp.float32).astype(
        jnp.bfloat16
    )
    value_columns = lax.all_to_all(value_rows, "ctx", split_axis=1, concat_axis=0, tiled=True)
    tap_columns = lax.all_to_all(filter_taps, "ctx", split_axis=1, concat_axis=0, tiled=True)
    channels_here = value_columns.shape[1]
    tables = column_tables(local_rows, peer_count)
    value_signal = value_columns.astype(jnp.float32).reshape(local_rows, peer_count, channels_here)
    tap_signal = tap_columns.astype(jnp.float32).reshape(local_rows, peer_count, channels_here)
    value_real, value_imag = column_spectrum(value_signal, tables)
    tap_real, tap_imag = column_spectrum(tap_signal, tables)
    product_real = value_real * tap_real - value_imag * tap_imag
    product_imag = value_real * tap_imag + value_imag * tap_real
    restored = column_inverse(product_real, product_imag, tables) / (2.0 * length)
    restored = restored.reshape(length, channels_here).astype(jnp.bfloat16)
    convolved = lax.all_to_all(restored, "ctx", split_axis=0, concat_axis=1, tiled=True)
    gated_rows = (convolved.astype(jnp.float32) * gate_rows.astype(jnp.float32)).astype(
        jnp.bfloat16
    )
    partial_sum = jnp.dot(gated_rows, out_weight, preferred_element_type=jnp.float32)
    own_sum = lax.psum_scatter(
        partial_sum.astype(jnp.bfloat16), "ch", scatter_dimension=1, tiled=True
    )
    return own_sum


LANES = 128
SHIFTS = 16
GROUP = 16
AHEAD_FLOPS = 4 * 2**30
NT = (((1,), (1,)), ((), ()))
TN = (((0,), (0,)), ((), ()))


def orders_kernel(flip_ref, mirror_ref):
    rows = flip_ref.shape[0]
    row = lax.broadcasted_iota(jnp.int32, (rows, rows), 0)
    column = lax.broadcasted_iota(jnp.int32, (rows, rows), 1)
    flip_ref[...] = jnp.where(row + column == rows - 1, 1.0, 0.0).astype(jnp.bfloat16)
    mirror_ref[...] = jnp.where(
        (row // GROUP == column // GROUP) & (row % GROUP + column % GROUP == GROUP - 1), 1.0, 0.0
    ).astype(jnp.bfloat16)


def orders(rows):
    shape = jax.ShapeDtypeStruct((rows, rows), jnp.bfloat16)
    return pl.pallas_call(
        orders_kernel,
        out_shape=[shape, shape],
        cost_estimate=pl.CostEstimate(
            flops=AHEAD_FLOPS, bytes_accessed=4 * rows * rows, transcendentals=0
        ),
        compiler_params=pltpu.CompilerParams(vmem_limit_bytes=4 * 2**20),
    )()


def turn_kernel(
    flip_ref, mirror_ref, tokens_ref, weight_ref, taps_ref, gate_ref, payload_ref, gate_t_ref
):
    peers, both, rows = payload_ref.shape
    part = both // 2
    value = jnp.dot(
        tokens_ref[...], weight_ref[...], preferred_element_type=jnp.float32
    ).astype(jnp.bfloat16)
    flipped = jnp.dot(flip_ref[...], taps_ref[...], preferred_element_type=jnp.float32)
    flipped_t = flipped.T.astype(jnp.bfloat16)
    value_t = jnp.concatenate(
        [
            lax.dot_general(
                mirror_ref[...], value[:, at : at + rows], NT, preferred_element_type=jnp.float32
            )
            for at in range(0, value.shape[1], rows)
        ],
        axis=0,
    ).astype(jnp.bfloat16)
    for peer in range(peers):
        payload_ref[peer, :part, :] = value_t[peer * part : (peer + 1) * part]
        payload_ref[peer, part:, :] = flipped_t[peer * part : (peer + 1) * part]
    gate_t_ref[...] = gate_ref[...].astype(jnp.float32).T.astype(jnp.bfloat16)


def turned(flip, mirror, tokens, value_weight, filter_taps, gate_rows, peers):
    rows, channels = filter_taps.shape
    return pl.pallas_call(
        turn_kernel,
        out_shape=[
            jax.ShapeDtypeStruct((peers, 2 * channels // peers, rows), jnp.bfloat16),
            jax.ShapeDtypeStruct((channels, rows), jnp.bfloat16),
        ],
        compiler_params=pltpu.CompilerParams(vmem_limit_bytes=24 * 2**20),
    )(flip, mirror, tokens, value_weight, filter_taps, gate_rows)


def conv_kernel(payload_ref, place_ref, out_ref, value_ref, taps_ref, packed_ref):
    blocks, both, lanes = payload_ref.shape
    channels = both // 2
    length = blocks * lanes
    outer = lanes // SHIFTS
    tail = jnp.zeros((GROUP, lanes), jnp.float32)
    sides = SHIFTS * GROUP // lanes
    slot = lax.broadcasted_iota(jnp.int32, (GROUP, lanes), 1) % GROUP
    def build(group):
        first = group * GROUP
        padded = jnp.concatenate(
            [
                payload_ref[q, first : first + GROUP, :].astype(jnp.float32)
                for q in range(blocks)
            ]
            + [tail],
            axis=1,
        )
        for shift in range(SHIFTS):
            moved = pltpu.roll(padded, shift, 1) if shift else padded
            value_ref[group, shift * GROUP : (shift + 1) * GROUP, :] = moved[:, :length].astype(
                jnp.bfloat16
            )
        padded = jnp.concatenate(
            [
                payload_ref[blocks - 1 - q, channels + first : channels + first + GROUP, :].astype(
                    jnp.float32
                )
                for q in range(blocks)
            ]
            + [tail],
            axis=1,
        )
        for k in range(outer):
            left = SHIFTS * (outer - 1 - k)
            moved = pltpu.roll(padded, length + lanes - left, 1) if left else padded
            taps_ref[group, k * GROUP : (k + 1) * GROUP, :length] = moved[:, :length].astype(
                jnp.bfloat16
            )
        taps_ref[group, :, length:] = jnp.zeros((outer * GROUP, lanes), jnp.bfloat16)

    def mix(group):
        for pair in range(blocks // 2):
            span = 2 * lanes * (pair + 1)
            even = (blocks - 1 - 2 * pair) * lanes
            odd = even - lanes
            left_side = jnp.concatenate(
                [
                    taps_ref[group, :, even : even + span],
                    taps_ref[group, :, odd : odd + span],
                ],
                axis=0,
            )
            mixed = lax.dot_general(
                left_side, value_ref[group, :, :span], NT, preferred_element_type=jnp.float32
            )
            for half in range(2):
                for side in range(sides):
                    packed = None
                    for k in range(outer):
                        at = (half * outer + k) * GROUP
                        tile = mixed[at : at + GROUP, side * lanes : (side + 1) * lanes]
                        tile = pltpu.roll(tile, k + 1, 1, stride=1, stride_axis=0)
                        packed = tile if k == 0 else jnp.where(slot == k, tile, packed)
                    at = (group * blocks + 2 * pair + half) * GROUP
                    packed_ref[at : at + GROUP, side * lanes : (side + 1) * lanes] = packed.astype(
                        jnp.bfloat16
                    )

    groups = channels // GROUP
    build(0)
    for group in range(groups):
        if group + 1 < groups:
            build(group + 1)
        mix(group)
    result = jnp.dot(packed_ref[...], place_ref[...], preferred_element_type=jnp.float32)
    result = result.astype(jnp.bfloat16)
    for group in range(channels // GROUP):
        for block in range(blocks):
            at = (group * blocks + block) * GROUP
            out_ref[block, group * GROUP : (group + 1) * GROUP, :] = result[at : at + GROUP]


def placement(lanes):
    per_side = lanes // GROUP
    side, place, slot, t = np.ix_(
        range(SHIFTS // per_side), range(per_side), range(GROUP), range(lanes)
    )
    r = side * per_side + (place - 1) % per_side
    hit = t == SHIFTS * slot + SHIFTS - 1 - r
    return jnp.asarray(hit.reshape(SHIFTS * GROUP, lanes), jnp.bfloat16)


def convolve(payload):
    blocks, both, lanes = payload.shape
    channels = both // 2
    groups = channels // GROUP
    outer = lanes // SHIFTS
    return pl.pallas_call(
        conv_kernel,
        out_shape=jax.ShapeDtypeStruct((blocks, channels, lanes), jnp.bfloat16),
        scratch_shapes=[
            pltpu.VMEM((groups, SHIFTS * GROUP, blocks * lanes), jnp.bfloat16),
            pltpu.VMEM((groups, outer * GROUP, (blocks + 1) * lanes), jnp.bfloat16),
            pltpu.VMEM((groups * blocks * GROUP, SHIFTS * GROUP), jnp.bfloat16),
        ],
        cost_estimate=pl.CostEstimate(
            flops=2 * channels * GROUP * (blocks * lanes) ** 2,
            bytes_accessed=6 * channels * blocks * lanes,
            transcendentals=0,
        ),
        compiler_params=pltpu.CompilerParams(vmem_limit_bytes=24 * 2**20),
    )(payload, placement(lanes))


def gate_kernel(conv_ref, gate_ref, out_ref):
    out_ref[...] = (
        conv_ref[...].astype(jnp.float32) * gate_ref[...].astype(jnp.float32)
    ).astype(out_ref.dtype)


def gated(conv_t, gate_t):
    return pl.pallas_call(
        gate_kernel,
        out_shape=jax.ShapeDtypeStruct(conv_t.shape, jnp.bfloat16),
        compiler_params=pltpu.CompilerParams(vmem_limit_bytes=4 * 2**20),
    )(conv_t, gate_t)


def project_kernel(flip, own_ref, weight_ref, out_ref):
    features = out_ref.shape[1]
    at = (lax.axis_index("ch") ^ flip) * features
    out_ref[...] = lax.dot_general(
        own_ref[...],
        weight_ref[:, pl.ds(pl.multiple_of(at, features), features)],
        TN,
        preferred_element_type=jnp.float32,
    ).astype(out_ref.dtype)


def project(own, weight, features, flip, dtype):
    depth, rows = own.shape
    return pl.pallas_call(
        functools.partial(project_kernel, flip),
        out_shape=jax.ShapeDtypeStruct((rows, features), dtype),
        cost_estimate=pl.CostEstimate(
            flops=2 * rows * depth * features,
            bytes_accessed=2 * depth * features + 4 * rows * features,
            transcendentals=0,
        ),
        compiler_params=pltpu.CompilerParams(vmem_limit_bytes=24 * 2**20),
    )(own, weight)


def add_kernel(first_ref, second_ref, out_ref):
    out_ref[...] = (first_ref[...] + second_ref[...].astype(jnp.float32)).astype(out_ref.dtype)


def added(first, second):
    return pl.pallas_call(
        add_kernel,
        out_shape=jax.ShapeDtypeStruct(first.shape, jnp.bfloat16),
        compiler_params=pltpu.CompilerParams(vmem_limit_bytes=8 * 2**20),
    )(first, second)


def by_blocks(tokens, value_weight, gate_rows, filter_taps, out_weight):
    peers = lax.axis_size("ctx")
    ranks = lax.axis_size("ch")
    features = out_weight.shape[1] // ranks
    near = [(i, i ^ 1) for i in range(ranks)]
    far = [(i, i ^ 2) for i in range(ranks)]
    flip, mirror = orders(tokens.shape[0])
    flip, tokens, value_weight, filter_taps, gate_rows = lax.optimization_barrier(
        (flip, tokens, value_weight, filter_taps, gate_rows)
    )
    payload, gate_t = turned(
        flip, mirror, tokens, value_weight, filter_taps, gate_rows, peers
    )
    payload = lax.all_to_all(payload, "ctx", split_axis=0, concat_axis=0, tiled=True)
    conv = convolve(payload)
    conv = lax.all_to_all(conv, "ctx", split_axis=0, concat_axis=0, tiled=True)
    own = gated(conv.reshape(gate_t.shape), gate_t)
    far_near = lax.ppermute(project(own, out_weight, features, 3, jnp.bfloat16), "ch", near)
    far_own = project(own, out_weight, features, 2, jnp.float32)
    sent = added(far_own, far_near)
    arrived = lax.ppermute(sent, "ch", far)
    kept_near = lax.ppermute(project(own, out_weight, features, 1, jnp.bfloat16), "ch", near)
    kept = project(own, out_weight, features, 0, jnp.float32)
    return (
        kept + kept_near.astype(jnp.float32) + arrived.astype(jnp.float32)
    ).astype(jnp.bfloat16)


def fits_blocks(tokens, value_weight, peers, ranks):
    rows, channels = tokens.shape[0], value_weight.shape[1]
    return (
        rows == LANES
        and ranks == 4
        and peers % 2 == 0
        and peers <= 16
        and channels % (peers * GROUP) == 0
    )


def on_device(tokens, value_weight, gate_rows, filter_taps, out_weight):
    peers, ranks = lax.axis_size("ctx"), lax.axis_size("ch")
    if fits_blocks(tokens, value_weight, peers, ranks):
        return by_blocks(tokens, value_weight, gate_rows, filter_taps, out_weight)
    return by_transform(tokens, value_weight, gate_rows, filter_taps, out_weight)


def solution(mesh):
    placed = (P("ctx", None), P(None, "ch"), P("ctx", "ch"), P("ctx", "ch"), P("ch", None))
    return jax.shard_map(
        on_device, mesh=mesh, in_specs=placed, out_specs=P("ctx", "ch"), check_vma=False
    )
```

```python
import functools
import math

import jax
import jax.numpy as jnp
import numpy as np
from jax import lax
from jax.experimental import pallas as pl
from jax.experimental.pallas import tpu as pltpu
from jax.sharding import PartitionSpec as P

HIGHEST = lax.Precision.HIGHEST


def column_tables(half_rows, peer_count):
    rows_full = 2 * half_rows
    length = rows_full * peer_count
    outer_freq = jnp.arange(rows_full, dtype=jnp.int32)[:, None]
    outer_pos = jnp.arange(half_rows, dtype=jnp.int32)[None, :]
    first_angle = (
        -2.0 * math.pi / rows_full * (outer_freq * outer_pos % rows_full).astype(jnp.float32)
    )
    inner_pos = jnp.arange(peer_count, dtype=jnp.int32)[None, :]
    twist_angle = -2.0 * math.pi / length * (outer_freq * inner_pos % length).astype(jnp.float32)
    inner_index = jnp.arange(peer_count, dtype=jnp.int32)
    second_angle = (
        -2.0
        * math.pi
        / peer_count
        * (inner_index[:, None] * inner_index[None, :] % peer_count).astype(jnp.float32)
    )
    return (
        jnp.cos(first_angle),
        jnp.sin(first_angle),
        jnp.cos(twist_angle),
        jnp.sin(twist_angle),
        jnp.cos(second_angle),
        jnp.sin(second_angle),
    )


def column_spectrum(signal, tables):
    first_cos, first_sin, twist_cos, twist_sin, second_cos, second_sin = tables
    section_real = jnp.einsum("kn,nbc->ckb", first_cos, signal, precision=HIGHEST)
    section_imag = jnp.einsum("kn,nbc->ckb", first_sin, signal, precision=HIGHEST)
    turned_real = section_real * twist_cos - section_imag * twist_sin
    turned_imag = section_real * twist_sin + section_imag * twist_cos

    def apply_second(table_part, operand):
        return jnp.einsum("ckb,bj->ckj", operand, table_part, precision=HIGHEST)

    spec_real = apply_second(second_cos, turned_real) - apply_second(second_sin, turned_imag)
    spec_imag = apply_second(second_sin, turned_real) + apply_second(second_cos, turned_imag)
    return (spec_real, spec_imag)


def column_inverse(spec_real, spec_imag, tables):
    first_cos, first_sin, twist_cos, twist_sin, second_cos, second_sin = tables

    def apply_second(table_part, operand):
        return jnp.einsum("ckj,bj->ckb", operand, table_part, precision=HIGHEST)

    back_real = apply_second(second_cos, spec_real) + apply_second(second_sin, spec_imag)
    back_imag = apply_second(second_cos, spec_imag) - apply_second(second_sin, spec_real)
    turned_real = back_real * twist_cos + back_imag * twist_sin
    turned_imag = back_imag * twist_cos - back_real * twist_sin
    return jnp.einsum("kn,ckb->nbc", first_cos, turned_real, precision=HIGHEST) + jnp.einsum(
        "kn,ckb->nbc", first_sin, turned_imag, precision=HIGHEST
    )


def by_transform(tokens, value_weight, gate_rows, filter_taps, out_weight):
    local_rows = tokens.shape[0]
    peer_count = lax.axis_size("ctx")
    length = peer_count * local_rows
    value_rows = jnp.dot(tokens, value_weight, preferred_element_type=jnp.float32).astype(
        jnp.bfloat16
    )
    value_columns = lax.all_to_all(value_rows, "ctx", split_axis=1, concat_axis=0, tiled=True)
    tap_columns = lax.all_to_all(filter_taps, "ctx", split_axis=1, concat_axis=0, tiled=True)
    channels_here = value_columns.shape[1]
    tables = column_tables(local_rows, peer_count)
    value_signal = value_columns.astype(jnp.float32).reshape(local_rows, peer_count, channels_here)
    tap_signal = tap_columns.astype(jnp.float32).reshape(local_rows, peer_count, channels_here)
    value_real, value_imag = column_spectrum(value_signal, tables)
    tap_real, tap_imag = column_spectrum(tap_signal, tables)
    product_real = value_real * tap_real - value_imag * tap_imag
    product_imag = value_real * tap_imag + value_imag * tap_real
    restored = column_inverse(product_real, product_imag, tables) / (2.0 * length)
    restored = restored.reshape(length, channels_here).astype(jnp.bfloat16)
    convolved = lax.all_to_all(restored, "ctx", split_axis=0, concat_axis=1, tiled=True)
    gated_rows = (convolved.astype(jnp.float32) * gate_rows.astype(jnp.float32)).astype(
        jnp.bfloat16
    )
    partial_sum = jnp.dot(gated_rows, out_weight, preferred_element_type=jnp.float32)
    own_sum = lax.psum_scatter(
        partial_sum.astype(jnp.bfloat16), "ch", scatter_dimension=1, tiled=True
    )
    return own_sum


LANES = 128
SHIFTS = 16
GROUP = 16
AHEAD_FLOPS = 4 * 2**30
NT = (((1,), (1,)), ((), ()))
TN = (((0,), (0,)), ((), ()))


def orders_kernel(flip_ref, mirror_ref):
    rows = flip_ref.shape[0]
    row = lax.broadcasted_iota(jnp.int32, (rows, rows), 0)
    column = lax.broadcasted_iota(jnp.int32, (rows, rows), 1)
    flip_ref[...] = jnp.where(row + column == rows - 1, 1.0, 0.0).astype(jnp.bfloat16)
    mirror_ref[...] = jnp.where(
        (row // GROUP == column // GROUP) & (row % GROUP + column % GROUP == GROUP - 1), 1.0, 0.0
    ).astype(jnp.bfloat16)


def orders(rows):
    shape = jax.ShapeDtypeStruct((rows, rows), jnp.bfloat16)
    return pl.pallas_call(
        orders_kernel,
        out_shape=[shape, shape],
        cost_estimate=pl.CostEstimate(
            flops=AHEAD_FLOPS, bytes_accessed=4 * rows * rows, transcendentals=0
        ),
        compiler_params=pltpu.CompilerParams(vmem_limit_bytes=4 * 2**20),
    )()


def turn_kernel(
    flip_ref, mirror_ref, tokens_ref, weight_ref, taps_ref, gate_ref, payload_ref, gate_t_ref
):
    peers, both, rows = payload_ref.shape
    part = both // 2
    value = jnp.dot(
        tokens_ref[...], weight_ref[...], preferred_element_type=jnp.float32
    ).astype(jnp.bfloat16)
    flipped = jnp.dot(flip_ref[...], taps_ref[...], preferred_element_type=jnp.float32)
    flipped_t = flipped.T.astype(jnp.bfloat16)
    value_t = jnp.concatenate(
        [
            lax.dot_general(
                mirror_ref[...], value[:, at : at + rows], NT, preferred_element_type=jnp.float32
            )
            for at in range(0, value.shape[1], rows)
        ],
        axis=0,
    ).astype(jnp.bfloat16)
    for peer in range(peers):
        payload_ref[peer, :part, :] = value_t[peer * part : (peer + 1) * part]
        payload_ref[peer, part:, :] = flipped_t[peer * part : (peer + 1) * part]
    gate_t_ref[...] = gate_ref[...].astype(jnp.float32).T.astype(jnp.bfloat16)


def turned(flip, mirror, tokens, value_weight, filter_taps, gate_rows, peers):
    rows, channels = filter_taps.shape
    return pl.pallas_call(
        turn_kernel,
        out_shape=[
            jax.ShapeDtypeStruct((peers, 2 * channels // peers, rows), jnp.bfloat16),
            jax.ShapeDtypeStruct((channels, rows), jnp.bfloat16),
        ],
        compiler_params=pltpu.CompilerParams(vmem_limit_bytes=24 * 2**20),
    )(flip, mirror, tokens, value_weight, filter_taps, gate_rows)


def conv_kernel(payload_ref, place_ref, out_ref, value_ref, taps_ref, packed_ref):
    blocks, both, lanes = payload_ref.shape
    channels = both // 2
    length = blocks * lanes
    outer = lanes // SHIFTS
    tail = jnp.zeros((GROUP, lanes), jnp.float32)
    sides = SHIFTS * GROUP // lanes
    slot = lax.broadcasted_iota(jnp.int32, (GROUP, lanes), 1) % GROUP
    def build(group):
        first = group * GROUP
        padded = jnp.concatenate(
            [
                payload_ref[q, first : first + GROUP, :].astype(jnp.float32)
                for q in range(blocks)
            ]
            + [tail],
            axis=1,
        )
        for shift in range(SHIFTS):
            moved = pltpu.roll(padded, shift, 1) if shift else padded
            value_ref[group, shift * GROUP : (shift + 1) * GROUP, :] = moved[:, :length].astype(
                jnp.bfloat16
            )
        padded = jnp.concatenate(
            [
                payload_ref[blocks - 1 - q, channels + first : channels + first + GROUP, :].astype(
                    jnp.float32
                )
                for q in range(blocks)
            ]
            + [tail],
            axis=1,
        )
        for k in range(outer):
            left = SHIFTS * (outer - 1 - k)
            moved = pltpu.roll(padded, length + lanes - left, 1) if left else padded
            taps_ref[group, k * GROUP : (k + 1) * GROUP, :length] = moved[:, :length].astype(
                jnp.bfloat16
            )
        taps_ref[group, :, length:] = jnp.zeros((outer * GROUP, lanes), jnp.bfloat16)

    def mix(group):
        for pair in range(blocks // 2):
            span = 2 * lanes * (pair + 1)
            even = (blocks - 1 - 2 * pair) * lanes
            odd = even - lanes
            left_side = jnp.concatenate(
                [
                    taps_ref[group, :, even : even + span],
                    taps_ref[group, :, odd : odd + span],
                ],
                axis=0,
            )
            mixed = lax.dot_general(
                left_side, value_ref[group, :, :span], NT, preferred_element_type=jnp.float32
            )
            for half in range(2):
                for side in range(sides):
                    packed = None
                    for k in range(outer):
                        at = (half * outer + k) * GROUP
                        tile = mixed[at : at + GROUP, side * lanes : (side + 1) * lanes]
                        tile = pltpu.roll(tile, k + 1, 1, stride=1, stride_axis=0)
                        packed = tile if k == 0 else jnp.where(slot == k, tile, packed)
                    at = (group * blocks + 2 * pair + half) * GROUP
                    packed_ref[at : at + GROUP, side * lanes : (side + 1) * lanes] = packed.astype(
                        jnp.bfloat16
                    )

    groups = channels // GROUP
    build(0)
    for group in range(groups):
        if group + 1 < groups:
            build(group + 1)
        mix(group)
    result = jnp.dot(packed_ref[...], place_ref[...], preferred_element_type=jnp.float32)
    result = result.astype(jnp.bfloat16)
    for group in range(channels // GROUP):
        for block in range(blocks):
            at = (group * blocks + block) * GROUP
            out_ref[block, group * GROUP : (group + 1) * GROUP, :] = result[at : at + GROUP]


def placement(lanes):
    per_side = lanes // GROUP
    side, place, slot, t = np.ix_(
        range(SHIFTS // per_side), range(per_side), range(GROUP), range(lanes)
    )
    r = side * per_side + (place - 1) % per_side
    hit = t == SHIFTS * slot + SHIFTS - 1 - r
    return jnp.asarray(hit.reshape(SHIFTS * GROUP, lanes), jnp.bfloat16)


def convolve(payload):
    blocks, both, lanes = payload.shape
    channels = both // 2
    groups = channels // GROUP
    outer = lanes // SHIFTS
    return pl.pallas_call(
        conv_kernel,
        out_shape=jax.ShapeDtypeStruct((blocks, channels, lanes), jnp.bfloat16),
        scratch_shapes=[
            pltpu.VMEM((groups, SHIFTS * GROUP, blocks * lanes), jnp.bfloat16),
            pltpu.VMEM((groups, outer * GROUP, (blocks + 1) * lanes), jnp.bfloat16),
            pltpu.VMEM((groups * blocks * GROUP, SHIFTS * GROUP), jnp.bfloat16),
        ],
        cost_estimate=pl.CostEstimate(
            flops=2 * channels * GROUP * (blocks * lanes) ** 2,
            bytes_accessed=6 * channels * blocks * lanes,
            transcendentals=0,
        ),
        compiler_params=pltpu.CompilerParams(vmem_limit_bytes=24 * 2**20),
    )(payload, placement(lanes))


def gate_kernel(conv_ref, gate_ref, weight_ref, own_ref, out_ref):
    own_ref[...] = (
        conv_ref[...].astype(jnp.float32) * gate_ref[...].astype(jnp.float32)
    ).astype(own_ref.dtype)
    project_kernel(3, own_ref, weight_ref, out_ref)


def gated(conv_t, gate_t, weight, features):
    return pl.pallas_call(
        gate_kernel,
        out_shape=[
            jax.ShapeDtypeStruct(conv_t.shape, jnp.bfloat16),
            jax.ShapeDtypeStruct((conv_t.shape[1], features), jnp.bfloat16),
        ],
        compiler_params=pltpu.CompilerParams(vmem_limit_bytes=24 * 2**20),
    )(conv_t, gate_t, weight)


def project_kernel(flip, own_ref, weight_ref, out_ref):
    features = out_ref.shape[1]
    at = (lax.axis_index("ch") ^ flip) * features
    out_ref[...] = lax.dot_general(
        own_ref[...],
        weight_ref[:, pl.ds(pl.multiple_of(at, features), features)],
        TN,
        preferred_element_type=jnp.float32,
    ).astype(out_ref.dtype)


def project(own, weight, features, flip, dtype):
    depth, rows = own.shape
    return pl.pallas_call(
        functools.partial(project_kernel, flip),
        out_shape=jax.ShapeDtypeStruct((rows, features), dtype),
        cost_estimate=pl.CostEstimate(
            flops=2 * rows * depth * features,
            bytes_accessed=2 * depth * features + 4 * rows * features,
            transcendentals=0,
        ),
        compiler_params=pltpu.CompilerParams(vmem_limit_bytes=24 * 2**20),
    )(own, weight)


def add_kernel(first_ref, second_ref, out_ref):
    out_ref[...] = (first_ref[...] + second_ref[...].astype(jnp.float32)).astype(out_ref.dtype)


def added(first, second):
    return pl.pallas_call(
        add_kernel,
        out_shape=jax.ShapeDtypeStruct(first.shape, jnp.bfloat16),
        compiler_params=pltpu.CompilerParams(vmem_limit_bytes=8 * 2**20),
    )(first, second)


def by_blocks(tokens, value_weight, gate_rows, filter_taps, out_weight):
    peers = lax.axis_size("ctx")
    ranks = lax.axis_size("ch")
    features = out_weight.shape[1] // ranks
    near = [(i, i ^ 1) for i in range(ranks)]
    far = [(i, i ^ 2) for i in range(ranks)]
    flip, mirror = orders(tokens.shape[0])
    flip, tokens, value_weight, filter_taps, gate_rows = lax.optimization_barrier(
        (flip, tokens, value_weight, filter_taps, gate_rows)
    )
    payload, gate_t = turned(
        flip, mirror, tokens, value_weight, filter_taps, gate_rows, peers
    )
    payload = lax.all_to_all(payload, "ctx", split_axis=0, concat_axis=0, tiled=True)
    conv = convolve(payload)
    conv = lax.all_to_all(conv, "ctx", split_axis=0, concat_axis=0, tiled=True)
    own, far_sent = gated(conv.reshape(gate_t.shape), gate_t, out_weight, features)
    far_near = lax.ppermute(far_sent, "ch", near)
    far_own = project(own, out_weight, features, 2, jnp.float32)
    sent = added(far_own, far_near)
    arrived = lax.ppermute(sent, "ch", far)
    kept_near = lax.ppermute(project(own, out_weight, features, 1, jnp.bfloat16), "ch", near)
    kept = project(own, out_weight, features, 0, jnp.float32)
    return (
        kept + kept_near.astype(jnp.float32) + arrived.astype(jnp.float32)
    ).astype(jnp.bfloat16)


def fits_blocks(tokens, value_weight, peers, ranks):
    rows, channels = tokens.shape[0], value_weight.shape[1]
    return (
        rows == LANES
        and ranks == 4
        and peers % 2 == 0
        and peers <= 16
        and channels % (peers * GROUP) == 0
    )


def on_device(tokens, value_weight, gate_rows, filter_taps, out_weight):
    peers, ranks = lax.axis_size("ctx"), lax.axis_size("ch")
    if fits_blocks(tokens, value_weight, peers, ranks):
        return by_blocks(tokens, value_weight, gate_rows, filter_taps, out_weight)
    return by_transform(tokens, value_weight, gate_rows, filter_taps, out_weight)


def solution(mesh):
    placed = (P("ctx", None), P(None, "ch"), P("ctx", "ch"), P("ctx", "ch"), P("ch", None))
    return jax.shard_map(
        on_device, mesh=mesh, in_specs=placed, out_specs=P("ctx", "ch"), check_vma=False
    )
```
